32 devices in a mesh: dp: 8 (over z, x), seq: 4 (over y, core).
Axes of the slice: x: 2, y: 2, z: 4, core: 2. Of those that a mesh axis runs over, the one named last changes fastest.
Arguments:
- inputs: bfloat16 [4, 8, 512, 384], P(None, 'dp', 'seq'), may hold values from -6 to 6
- lengths: int32 [4, 8], P(None, 'dp'), may hold values from 1 to 512, as said below
- cotangent: bfloat16 [4, 8, 512, 384], P(None, 'dp', 'seq'), may hold values from -6 to 6
- pool_cotangent: bfloat16 [4, 8, 384], P(None, 'dp'), may hold values from -24 to 24
- qkv_weight: bfloat16 [384, 1152], replicated, may hold values from -0.4375 to 0.4375
- query_bias: float32 [384], replicated, may hold values from -3 to 3
- value_bias: float32 [384], replicated, may hold values from -3 to 3
- out_weight: bfloat16 [384, 384], replicated, may hold values from -1.75 to 1.75
- out_bias: float32 [384], replicated, may hold values from -3 to 3
- norm1_gain: float32 [384], replicated, may hold values from 0.5 to 1.5
- norm1_bias: float32 [384], replicated, may hold values from -2 to 2
- up_weight: bfloat16 [384, 1536], replicated, may hold values from -0.3125 to 0.3125
- up_bias: float32 [1536], replicated, may hold values from -3 to 3
- down_weight: bfloat16 [1536, 384], replicated, may hold values from -0.21875 to 0.21875
- down_bias: float32 [384], replicated, may hold values from -3 to 3
- norm2_gain: float32 [384], replicated, may hold values from 0.5 to 1.5
- norm2_bias: float32 [384], replicated, may hold values from -2 to 2
Outputs:
- block_out: bfloat16 [4, 8, 512, 384], P(None, 'dp', 'seq')
- pooled: float32 [4, 8, 384], P(None, 'dp')
- input_grad: bfloat16 [4, 8, 512, 384], P(None, 'dp', 'seq')
- grad_qkv_weight: float32 [384, 1152], replicated
- grad_query_bias: float32 [384], replicated
- grad_value_bias: float32 [384], replicated
- grad_out_weight: float32 [384, 384], replicated
- grad_out_bias: float32 [384], replicated
- grad_norm1_gain: float32 [384], replicated
- grad_norm1_bias: float32 [384], replicated
- grad_up_weight: float32 [384, 1536], replicated
- grad_up_bias: float32 [1536], replicated
- grad_down_weight: float32 [1536, 384], replicated
- grad_down_bias: float32 [384], replicated
- grad_norm2_gain: float32 [384], replicated
- grad_norm2_bias: float32 [384], replicated
The draws below stay inside these ranges and needn't reach their ends.
Inputs may be any that keep to these rules, and one draw needn't show every extreme that they name: `lengths`: for every sequence index, at least one of the 4 micro-batches has length 512.
All inputs are finite; a program needn't handle non-finite values.
Results may differ from the reference program's by a relative error of at most 0.015.
The reference program's roundings to bfloat16 on the way count: a program that leaves them out, or rounds other values in their place, can miss the bound.
Values may be sent and summed in bfloat16 or wider, within the bound.
A program may use at most 128 MiB of HBM per device.

```python
import math
import jax
import jax.numpy as jnp
from jax import lax

D = 384
H = 12
HD = 32
FF = 1536
LEN = 512
MICRO = 4
SEQS = 8


def draw_lengths(key, part):
    key = jax.random.fold_in(key, 11)
    key_kind, key_short, key_long, key_full = jax.random.split(key, 4)
    kinds = jax.random.randint(key_kind, (MICRO, SEQS), 0, 3)
    short = jax.random.randint(key_short, (MICRO, SEQS), 1, LEN // 4 + 1)
    longer = jax.random.randint(key_long, (MICRO, SEQS), LEN // 2, LEN + 1)
    drawn = jnp.where(kinds == 0, short, longer)
    chosen = jax.random.randint(key_full, (1, SEQS), 0, MICRO)
    micro_ids = jnp.arange(MICRO)[:, None]
    full_slot = micro_ids == chosen
    return jnp.where(full_slot, LEN, drawn).astype(jnp.int32)


def block_scale(stream_key, shape, cuts, smallest, top_value):
    factor_of, own = 1.0, jax.random.fold_in(stream_key, 6)
    for position, shards_of in cuts:
        draws = jnp.exp(jax.random.uniform(jax.random.fold_in(own, position), (shards_of,), jnp.float32, smallest / len(cuts), top_value / len(cuts)))
        factor_of = factor_of * jnp.repeat(draws, shape[position] // shards_of).reshape([-1 if axis == position else 1 for axis in range(len(shape))])
    return factor_of


def scatter_about(key, extent, deviation, reach, pieces=(), held_as=jnp.bfloat16):
    values = deviation * jax.random.normal(key, extent, jnp.float32)
    if pieces:
        values = values * block_scale(key, extent, pieces, -0.22, 0.18)
    return jnp.clip(values, -reach, reach).astype(held_as)


def setup_inputs(seed: int = 0) -> dict:
    splits = jax.random.split(jax.random.key(seed), 18)
    inputs = scatter_about(splits[0], (MICRO, SEQS, LEN, D), 1.0, 6.0, ((1, 8), (2, 4)))
    lengths = draw_lengths(jax.random.fold_in(splits[17], 71), 0)
    cotangent = scatter_about(splits[2], (MICRO, SEQS, LEN, D), 1.0, 6.0, ((1, 8), (2, 4)))
    pool_cotangent = scatter_about(splits[3], (MICRO, SEQS, D), 4.0, 24.0, ((1, 8),))
    qkv_weight = scatter_about(splits[4], (D, 3 * D), (D // 2) ** -0.5, 0.4375)
    query_bias = scatter_about(splits[5], (D,), 0.5, 3.0, (), jnp.float32)
    value_bias = scatter_about(splits[6], (D,), 0.5, 3.0, (), jnp.float32)
    out_weight = scatter_about(splits[7], (D, D), (max(D // 32, 1)) ** -0.5, 1.75)
    out_bias = scatter_about(splits[8], (D,), 0.5, 3.0, (), jnp.float32)
    norm1_gain = jnp.clip(1.0 + 0.1 * jax.random.normal(splits[9], (D,), jnp.float32), 0.5, 1.5)
    norm1_bias = scatter_about(splits[10], (D,), 0.3, 2.0, (), jnp.float32)
    up_weight = scatter_about(splits[11], (D, FF), D ** -0.5, 0.3125)
    up_bias = scatter_about(splits[12], (FF,), 0.5, 3.0, (), jnp.float32)
    down_weight = scatter_about(splits[13], (FF, D), (FF // 2) ** -0.5, 0.21875)
    down_bias = scatter_about(splits[14], (D,), 0.5, 3.0, (), jnp.float32)
    norm2_gain = jnp.clip(1.0 + 0.1 * jax.random.normal(splits[15], (D,), jnp.float32), 0.5, 1.5)
    norm2_bias = scatter_about(splits[16], (D,), 0.3, 2.0, (), jnp.float32)
    return dict(inputs=inputs, lengths=lengths, cotangent=cotangent, pool_cotangent=pool_cotangent, qkv_weight=qkv_weight, query_bias=query_bias, value_bias=value_bias, out_weight=out_weight, out_bias=out_bias, norm1_gain=norm1_gain, norm1_bias=norm1_bias, up_weight=up_weight, up_bias=up_bias, down_weight=down_weight, down_bias=down_bias, norm2_gain=norm2_gain, norm2_bias=norm2_bias)


epsilon = 1e-06
highest = lax.Precision.HIGHEST

@jax.custom_vjp
def low(v):
    return lax.optimization_barrier(v.astype(jnp.bfloat16)).astype(jnp.float32)

@jax.custom_vjp
def low_back(v):
    return v

def low_keep(v):
    return (low(v), None)

def low_pass(kept, grad):
    return (grad,)

def back_keep(v):
    return (v, None)

def back_low(kept, grad):
    return (low(grad),)
low.defvjp(low_keep, low_pass)
low_back.defvjp(back_keep, back_low)

def layer_norm(values, scale_gain, shift):
    centre = values - lax.optimization_barrier(jnp.mean(values, axis=-1, keepdims=True))
    inverse = lax.rsqrt(lax.optimization_barrier(jnp.mean(centre * centre, axis=-1, keepdims=True)) + epsilon)
    return centre * inverse * scale_gain + shift

def forward(params, inputs, lengths):
    qkv_weight, query_bias, value_bias, out_weight, out_bias, norm1_gain, norm1_bias, up_weight, up_bias, down_weight, down_bias, norm2_gain, norm2_bias = params
    groups = inputs.shape[0]
    flat = inputs.reshape(groups * LEN, D)
    projected = jnp.dot(flat, qkv_weight, precision=highest)
    joined = jnp.concatenate([projected[:, :D] + query_bias, projected[:, D:2 * D], projected[:, 2 * D:] + value_bias], axis=1)
    joined = low(low_back(joined)).reshape(groups, LEN, 3, H, HD)
    scores = jnp.einsum('gqhd,gkhd->ghqk', joined[:, :, 0], joined[:, :, 1], precision=highest) * HD ** (-0.5)
    scores = low_back(scores)
    valid = jnp.arange(LEN)[None, :] < lengths[:, None]
    scores = jnp.where(valid[:, None, None, :], scores, -1e+30)
    weights = low(jax.nn.softmax(scores, axis=-1))
    context = jnp.einsum('ghqk,gkhd->gqhd', weights, joined[:, :, 2], precision=highest)
    context = low(low_back(context.reshape(groups * LEN, D)))
    attended = low_back(jnp.dot(context, out_weight, precision=highest) + out_bias)
    first = layer_norm(flat + attended, norm1_gain, norm1_bias)
    upper = low_back(jnp.dot(low(first), up_weight, precision=highest) + up_bias)
    active = low(jax.nn.gelu(upper, approximate=False))
    lower = low_back(jnp.dot(active, down_weight, precision=highest) + down_bias)
    second = layer_norm(first + lower, norm2_gain, norm2_bias)
    keep_rows = valid.reshape(groups * LEN, 1)
    result = jnp.where(keep_rows, second, jnp.zeros_like(second)).reshape(groups, LEN, D)
    pooled = lax.optimization_barrier(jnp.sum(result, axis=1)) / lengths[:, None].astype(result.dtype)
    return (result, pooled)

def reference(inputs, lengths, cotangent, pool_cotangent, qkv_weight, query_bias, value_bias, out_weight, out_bias, norm1_gain, norm1_bias, up_weight, up_bias, down_weight, down_bias, norm2_gain, norm2_bias):
    params = tuple((item.astype(jnp.float32) for item in (qkv_weight, query_bias, value_bias, out_weight, out_bias, norm1_gain, norm1_bias, up_weight, up_bias, down_weight, down_bias, norm2_gain, norm2_bias)))
    block = math.gcd(SEQS, max(1, 4096 // LEN))
    blocks = MICRO * SEQS // block
    rows_all = inputs.astype(jnp.float32).reshape(blocks, block, LEN, D)
    spans_all = lengths.reshape(blocks, block)
    grads_all = cotangent.astype(jnp.float32).reshape(blocks, block, LEN, D)
    pools_all = pool_cotangent.astype(jnp.float32).reshape(blocks, block, D)

    def step_block(carry, items):
        rows_in, spans, grad_rows, grad_pool = items
        outputs, pullback = jax.vjp(lambda weights_in, values_in: forward(weights_in, values_in, spans), params, rows_in)
        grad_params, grad_inputs = pullback((grad_rows, grad_pool))
        carry = jax.tree.map(lambda left, right: left + right, carry, grad_params)
        return (carry, (outputs[0].astype(jnp.bfloat16), outputs[1], grad_inputs.astype(jnp.bfloat16)))
    start = jax.tree.map(jnp.zeros_like, params)
    sums, stacked = lax.scan(step_block, start, (rows_all, spans_all, grads_all, pools_all))
    return (stacked[0].reshape(MICRO, SEQS, LEN, D), stacked[1].reshape(MICRO, SEQS, D), stacked[2].reshape(MICRO, SEQS, LEN, D), sums[0], sums[1], sums[2], sums[3], sums[4], sums[5], sums[6], sums[7], sums[8], sums[9], sums[10], sums[11], sums[12])
```

```python
import functools

import jax
import jax.numpy as jnp
from jax import lax
from jax.experimental import pallas as pl
from jax.experimental.pallas import tpu as pltpu
from jax.sharding import PartitionSpec as P

H = 12
HD = 32
D = 384
FF = 1536
EPS = 1e-6
F32 = jnp.float32
BF16 = jnp.bfloat16
MESH = pl.DeviceIdType.MESH
NN = (((1,), (0,)), ((), ()))
NT = (((1,), (1,)), ((), ()))
TN = (((0,), (0,)), ((), ()))
LOG2E = 1.4426950408889634
SCALE = HD**-0.5
VROWS = HD + 16
CHUNKS = 3
ROWS = 1536


def dot(left, right, dims):
    return lax.dot_general(left, right, dims, preferred_element_type=F32)


def gelu_and_slope(upper):
    cdf = 0.5 * (1.0 + lax.erf(upper * 2.0**-0.5))
    density = jnp.exp2((-0.5 * LOG2E) * (upper * upper)) * (2.0 * jnp.pi) ** -0.5
    return upper * cdf, cdf + upper * density


def layer_norm(values):
    centre = values - jnp.mean(values, axis=-1, keepdims=True)
    inverse = lax.rsqrt(jnp.mean(centre * centre, axis=-1, keepdims=True) + EPS)
    return centre * inverse, inverse


def norm_back(grad_out, normal, inverse, gain):
    scaled = grad_out * gain
    return inverse * (
        scaled
        - jnp.mean(scaled, axis=-1, keepdims=True)
        - normal * jnp.mean(scaled * normal, axis=-1, keepdims=True)
    )


def kernel(
    ndp,
    inputs_ref, lengths_ref, cot_ref, pool_ref,
    qkv_hbm, qb_ref, vb_ref, out_hbm, ob_ref, g1_ref, b1_ref,
    up_hbm, ub_ref, down_hbm, db_ref, g2_ref, b2_ref,
    block_ref, pooled_ref, igrad_ref, grads_ref, small_ref,
    x, cot, qkv_w, out_w, up_w, down_w, qkv_t, x_t,
    q_t, kd_t, kz_t, v_x, probs, inv, c_t, y1, r1, first_low, active, slope,
    lower, gsum, g_low, g_up, g_hid, gc_t, gj_t, bout, igr, pool,
    part, got0, got1, got2, got3, shard1, shard2, shard3, full, small, small_got,
    w_sem, loc_sem, in_send, in_recv, out_send, out_recv, pool_send, pool_recv,
    rs_send, rs_recv, ag_send, ag_recv, sm_send, sm_recv, fin_sem,
):
    dp = lax.axis_index("dp")
    sq = lax.axis_index("seq")
    core = lax.rem(sq, 2)
    yy = lax.div(sq, 2)
    xx = lax.rem(dp, 2)
    zz = lax.rem(lax.div(dp, 2), 4)
    extra = []
    bit = 8
    while bit < ndp:
        extra.append(bit)
        bit *= 2

    def flip(index, amount):
        digit = lax.rem(lax.div(index, amount), 2)
        return index + amount * (1 - 2 * digit)

    seq_peers = [lax.rem(sq + step, 4) for step in (1, 2, 3)]
    core_peer = (dp, flip(sq, 1))
    y_peer = (dp, flip(sq, 2))
    x_peer = (flip(dp, 1), sq)
    z_ids = [lax.rem(zz + step, 4) for step in (1, 2, 3)]
    z_peers = [(dp + 2 * (other - zz), sq) for other in z_ids]
    w_peers = [(flip(dp, amount), sq) for amount in extra]
    greeted = [(dp, peer) for peer in seq_peers] + [x_peer] + z_peers + w_peers

    loads = [
        pltpu.make_async_copy(src, dst, w_sem.at[i])
        for i, (src, dst) in enumerate(
            [(qkv_hbm, qkv_w), (out_hbm, out_w), (up_hbm, up_w), (down_hbm, down_w)]
        )
    ]
    for load in loads:
        load.start()
    own_rows = pl.ds(pl.multiple_of(sq * 128, 128), 128)
    own_x = pltpu.make_async_copy(inputs_ref.at[sq, 0], x.at[own_rows], loc_sem.at[0])
    own_c = pltpu.make_async_copy(cot_ref.at[sq, 0], cot.at[own_rows], loc_sem.at[1])
    own_x.start()
    own_c.start()

    barrier = pltpu.get_barrier_semaphore()
    for peer in greeted:
        pl.semaphore_signal(barrier, inc=1, device_id=peer, device_id_type=MESH)
    pl.semaphore_wait(barrier, len(greeted))

    def remote(src, dst, send, recv, peer):
        return pltpu.make_async_remote_copy(
            src_ref=src, dst_ref=dst, send_sem=send, recv_sem=recv,
            device_id=peer, device_id_type=MESH,
        )

    x_moves, c_moves = [], []
    for which, (src, dst, moves) in enumerate(((inputs_ref, x, x_moves), (cot_ref, cot, c_moves))):
        for i, peer in enumerate(seq_peers):
            move = remote(
                src.at[peer, 0], dst.at[own_rows],
                in_send.at[which, i], in_recv.at[which, i], (dp, peer),
            )
            move.start()
            moves.append(move)

    span = lengths_ref[sq, 0]
    count = span.astype(F32)
    lane_valid = lax.broadcasted_iota(jnp.int32, (1, 512), 1) < span

    loads[0].wait()

    def turn(i, carry):
        cols = pl.ds(pl.multiple_of(i * 128, 128), 128)
        qkv_t[cols, :] = qkv_w[:, cols].T
        return carry

    lax.fori_loop(0, 9, turn, 0)
    own_x.wait()
    for move in x_moves:
        move.wait()

    x_t[:D, :] = x[...].T
    x_t[D:, :] = jnp.ones((16, 512), BF16)

    qcol = jnp.broadcast_to(qb_ref[...], (8, D)).T[:, :1]
    vcol = jnp.broadcast_to(vb_ref[...], (8, D)).T[:, :1]
    q_t[...] = (dot(qkv_t[:D, :], x[...], NT) + qcol).astype(BF16)
    keys = dot(qkv_t[D : 2 * D, :], x[...], NT)
    kd_t[...] = jnp.where(lane_valid, keys, keys[:, :1]).astype(BF16)
    kz_t[...] = jnp.where(lane_valid, keys, 0.0).astype(BF16)
    values = jnp.where(lane_valid, dot(qkv_t[2 * D :, :], x[...], NT) + vcol, 0.0).astype(BF16)
    ones_row = jnp.broadcast_to(jnp.where(lane_valid, 1.0, 0.0), (16, 512)).astype(BF16)
    for h in range(H):
        v_x[h * VROWS : h * VROWS + HD, :] = values[h * HD : (h + 1) * HD, :]
        v_x[h * VROWS + HD : (h + 1) * VROWS, :] = ones_row

    def attend(h, carry):
        rows = pl.ds(pl.multiple_of(h * HD, HD), HD)
        scores = dot(kd_t[rows, :], q_t[rows, :], TN)
        peak = jnp.max(scores, axis=0, keepdims=True)
        raised = jnp.exp2(scores * (SCALE * LOG2E) - peak * (SCALE * LOG2E)).astype(BF16)
        probs[h] = raised
        both = dot(v_x[pl.ds(pl.multiple_of(h * VROWS, 16), VROWS), :], raised, NN)
        inverse = 1.0 / both[HD : HD + 1, :]
        inv[h] = jnp.broadcast_to(inverse, (8, 512))
        c_t[rows, :] = (both[:HD, :] * inverse).astype(BF16)
        return carry

    lax.fori_loop(0, H, attend, 0)

    loads[1].wait()

    def rows_of(i, size):
        return pl.ds(pl.multiple_of(i * size, size), size)

    lower[...] = dot(c_t[...], out_w[...], TN)

    def norm_one(i, carry):
        rows = rows_of(i, 128)
        normal, inverse = layer_norm(x[rows, :].astype(F32) + lower[rows, :] + ob_ref[...])
        y1[rows, :] = normal
        r1[rows, :] = inverse
        first_low[rows, :] = (normal * g1_ref[...] + b1_ref[...]).astype(BF16)
        return carry

    lax.fori_loop(0, 4, norm_one, 0)
    loads[2].wait()

    def raise_up(i, carry):
        cols = rows_of(i, 256)
        upper = dot(first_low[...], up_w[:, cols], NN) + ub_ref[:, cols]
        act, slp = gelu_and_slope(upper)
        active[:, cols] = act.astype(BF16)
        slope[:, cols] = slp
        return carry

    lax.fori_loop(0, FF // 256, raise_up, 0)
    loads[3].wait()
    lower[...] = dot(active[...], down_w[...], NN)
    own_c.wait()
    for move in c_moves:
        move.wait()
    pool_share = pool_ref[sq].astype(F32) / count

    zero_row = jnp.zeros((1, D), F32)

    def norm_two(i, carry):
        sums, gain_sum, bias_sum, down_sum = carry
        rows = rows_of(i, 128)
        firsts = y1[rows, :] * g1_ref[...] + b1_ref[...]
        normal, inverse = layer_norm(firsts + lower[rows, :] + db_ref[...])
        here = lax.broadcasted_iota(jnp.int32, (128, 1), 0) + i * 128 < span
        masked = jnp.where(here, normal * g2_ref[...] + b2_ref[...], 0.0)
        bout[rows, :] = masked.astype(BF16)
        grad = jnp.where(here, cot[rows, :].astype(F32) + pool_share, 0.0)
        grad_in = norm_back(grad, normal, inverse, g2_ref[...])
        gsum[rows, :] = grad_in
        low = grad_in.astype(BF16)
        g_low[rows, :] = low
        return (
            sums + jnp.sum(masked, axis=0, keepdims=True),
            gain_sum + jnp.sum(grad * normal, axis=0, keepdims=True),
            bias_sum + jnp.sum(grad, axis=0, keepdims=True),
            down_sum + jnp.sum(low.astype(F32), axis=0, keepdims=True),
        )

    sums, gain2, bias2, down_sum = lax.fori_loop(
        0, 4, norm_two, (zero_row, zero_row, zero_row, zero_row)
    )
    pool[sq] = jnp.broadcast_to(sums / count, (8, D))
    small[4:5, :] = down_sum
    small[10:11, :] = gain2
    small[11:12, :] = bias2

    out_moves = []
    for i, peer in enumerate(seq_peers):
        move = remote(
            bout.at[pl.ds(pl.multiple_of(peer * 128, 128), 128)], block_ref.at[sq, 0],
            out_send.at[0, i], out_recv.at[0, i], (dp, peer),
        )
        move.start()
        out_moves.append(move)
        move = remote(pool.at[sq], pool.at[sq], pool_send.at[i], pool_recv.at[i], (dp, peer))
        move.start()
        out_moves.append(move)
    own_b = pltpu.make_async_copy(bout.at[own_rows], block_ref.at[sq, 0], loc_sem.at[2])
    own_b.start()

    part[0] = dot(active[...], g_low[...], TN).astype(BF16)

    def back_up(i, carry):
        cols = rows_of(i, 256)
        low = (dot(g_low[...], down_w[cols, :], NT) * slope[:, cols]).astype(BF16)
        g_up[:, cols] = low
        return carry

    lax.fori_loop(0, FF // 256, back_up, 0)
    for i in range(4):
        small[i : i + 1, :] = jnp.sum(
            g_up[:, i * D : (i + 1) * D].astype(F32), axis=0, keepdims=True
        )
        part[1, i * D : (i + 1) * D, :] = dot(
            first_low[...], g_up[:, i * D : (i + 1) * D], TN
        ).astype(BF16)
    lower[...] = dot(g_up[...], up_w[...], NT)

    def norm_one_back(i, carry):
        gain_sum, bias_sum, out_sum = carry
        rows = rows_of(i, 128)
        grad = gsum[rows, :] + lower[rows, :]
        normal = y1[rows, :]
        grad_in = norm_back(grad, normal, r1[rows, :], g1_ref[...])
        g_hid[rows, :] = grad_in
        low = grad_in.astype(BF16)
        g_low[rows, :] = low
        return (
            gain_sum + jnp.sum(grad * normal, axis=0, keepdims=True),
            bias_sum + jnp.sum(grad, axis=0, keepdims=True),
            out_sum + jnp.sum(low.astype(F32), axis=0, keepdims=True),
        )

    gain1, bias1, out_sum = lax.fori_loop(0, 4, norm_one_back, (zero_row, zero_row, zero_row))
    small[5:6, :] = out_sum
    small[8:9, :] = gain1
    small[9:10, :] = bias1
    small[12:16, :] = jnp.zeros((4, D), F32)

    part[2, :D, :] = dot(c_t[...], g_low[...], NN).astype(BF16)
    gc_t[...] = dot(out_w[...], g_low[...], NT).astype(BF16)

    def attend_back(h, carry):
        rows = pl.ds(pl.multiple_of(h * HD, HD), HD)
        inverse = inv[h][:1, :]
        grad_c = (gc_t[rows, :].astype(F32) * inverse).astype(BF16)
        inner = jnp.sum(grad_c.astype(F32) * c_t[rows, :].astype(F32), axis=0, keepdims=True)
        grad_w = dot(v_x[pl.ds(pl.multiple_of(h * VROWS, 16), HD), :], grad_c, TN)
        weights = probs[h]
        grad_s = (weights.astype(F32) * (grad_w - inner)).astype(BF16)
        gj_t[rows, :] = (dot(kz_t[rows, :], grad_s, NN) * SCALE).astype(BF16)
        gk = jnp.where(lane_valid, dot(q_t[rows, :], grad_s, NT) * SCALE, 0.0)
        gj_t[pl.ds(pl.multiple_of(D + h * HD, HD), HD), :] = gk.astype(BF16)
        gv = jnp.where(lane_valid, dot(grad_c, weights, NT), 0.0)
        gj_t[pl.ds(pl.multiple_of(2 * D + h * HD, HD), HD), :] = gv.astype(BF16)
        return carry

    lax.fori_loop(0, H, attend_back, 0)

    for j in range(3):
        both = dot(x_t[...], gj_t[j * D : (j + 1) * D, :], NT)
        part[2, (j + 1) * D : (j + 2) * D, :] = both[:D, :].astype(BF16)
        if j == 0:
            small[6:7, :] = both[D : D + 1, :]
        if j == 2:
            small[7:8, :] = both[D : D + 1, :]
    igr[...] = (g_hid[...] + dot(gj_t[...], qkv_t[...], TN)).astype(BF16)
    for i, peer in enumerate(seq_peers):
        move = remote(
            igr.at[pl.ds(pl.multiple_of(peer * 128, 128), 128)], igrad_ref.at[sq, 0],
            out_send.at[1, i], out_recv.at[1, i], (dp, peer),
        )
        move.start()
        out_moves.append(move)
    own_i = pltpu.make_async_copy(igr.at[own_rows], igrad_ref.at[sq, 0], loc_sem.at[3])
    own_i.start()

    items = [(chunk, colour) for chunk in range(CHUNKS) for colour in range(3)]

    def lanes(colour):
        return pl.ds(colour * 128, 128)

    def piece(base, size):
        return pl.ds(pl.multiple_of(base, 16), size)

    half, quarter, eighth, unit = ROWS // 2, ROWS // 4, ROWS // 8, ROWS // 32

    def orders(colour):
        if colour == 0:
            return (yy, y_peer), (xx, x_peer)
        return (xx, x_peer), (yy, y_peer)

    def small_step(step, peer):
        move = remote(small, small_got.at[step], sm_send.at[step], sm_recv.at[step], peer)
        move.start()
        move.wait()
        small[...] = small[...] + small_got[step]

    moves = []
    for n, (chunk, colour) in enumerate(items):
        move = remote(
            part.at[chunk, piece((1 - core) * half, half), lanes(colour)],
            got0.at[chunk, :, lanes(colour)], rs_send.at[0, n], rs_recv.at[0, n], core_peer,
        )
        move.start()
        moves.append(move)
    small_step(0, core_peer)
    stage = []
    for n, (chunk, colour) in enumerate(items):
        moves[n].wait()
        shard1[chunk, :, lanes(colour)] = (
            part[chunk, piece(core * half, half), lanes(colour)].astype(F32)
            + got0[chunk, :, lanes(colour)].astype(F32)
        ).astype(BF16)
        (digit, peer), _ = orders(colour)
        move = remote(
            shard1.at[chunk, piece((1 - digit) * quarter, quarter), lanes(colour)],
            got1.at[chunk, :, lanes(colour)], rs_send.at[1, n], rs_recv.at[1, n], peer,
        )
        move.start()
        stage.append(move)
    small_step(1, y_peer)
    moves, stage = stage, []
    for n, (chunk, colour) in enumerate(items):
        moves[n].wait()
        (digit, _), (digit2, peer) = orders(colour)
        shard2[chunk, :, lanes(colour)] = (
            shard1[chunk, piece(digit * quarter, quarter), lanes(colour)].astype(F32)
            + got1[chunk, :, lanes(colour)].astype(F32)
        ).astype(BF16)
        move = remote(
            shard2.at[chunk, piece((1 - digit2) * eighth, eighth), lanes(colour)],
            got2.at[chunk, :, lanes(colour)], rs_send.at[2, n], rs_recv.at[2, n], peer,
        )
        move.start()
        stage.append(move)
    small_step(2, x_peer)
    moves, stage = stage, []
    for n, (chunk, colour) in enumerate(items):
        moves[n].wait()
        _, (digit2, _) = orders(colour)
        shard3[chunk, :, lanes(colour)] = (
            shard2[chunk, piece(digit2 * eighth, eighth), lanes(colour)].astype(F32)
            + got2[chunk, :, lanes(colour)].astype(F32)
        ).astype(BF16)
        for j in range(3):
            move = remote(
                shard3.at[chunk, piece(z_ids[j] * unit, unit), lanes(colour)],
                got3.at[chunk, j, :, lanes(colour)],
                rs_send.at[3 + j, n], rs_recv.at[3 + j, n], z_peers[j],
            )
            move.start()
            stage.append(move)
    z_moves = []
    for j in range(3):
        move = remote(small, small_got.at[3 + j], sm_send.at[3 + j], sm_recv.at[3 + j], z_peers[j])
        move.start()
        z_moves.append(move)
    for move in z_moves:
        move.wait()
    parts4 = [small[...]] + [small_got[3 + j] for j in range(3)]

    def by_place(place):
        total = None
        for j in range(4):
            term = jnp.where(lax.rem(zz - j + 4, 4) == place, parts4[j], 0.0)
            total = term if total is None else total + term
        return total

    small[...] = (by_place(0) + by_place(1)) + (by_place(2) + by_place(3))
    for e, peer in enumerate(w_peers):
        small_step(6 + e, peer)

    moves, stage = stage, []
    for n, (chunk, colour) in enumerate(items):
        total = shard3[chunk, piece(zz * unit, unit), lanes(colour)].astype(F32)
        for j in range(3):
            moves[3 * n + j].wait()
            total = total + got3[chunk, j, :, lanes(colour)].astype(F32)
        (digit, _), (digit2, _) = orders(colour)
        base = core * half + digit * quarter + digit2 * eighth
        mine = piece(base + zz * unit, unit)
        full[chunk, mine, lanes(colour)] = total.astype(BF16)
        for e, peer in enumerate(w_peers):
            move = remote(
                full.at[chunk, mine, lanes(colour)],
                got3.at[chunk, 3 + e, :, lanes(colour)],
                rs_send.at[6 + e, n], rs_recv.at[6 + e, n], peer,
            )
            move.start()
            move.wait()
            full[chunk, mine, lanes(colour)] = (
                full[chunk, mine, lanes(colour)].astype(F32)
                + got3[chunk, 3 + e, :, lanes(colour)].astype(F32)
            ).astype(BF16)
        for j in range(3):
            spot = full.at[chunk, mine, lanes(colour)]
            move = remote(spot, spot, ag_send.at[3 + j, n], ag_recv.at[3 + j, n], z_peers[j])
            move.start()
            stage.append(move)
    moves, stage = stage, []
    for n, (chunk, colour) in enumerate(items):
        for j in range(3):
            moves[3 * n + j].wait()
        (digit, _), (digit2, peer) = orders(colour)
        spot = full.at[chunk, piece(core * half + digit * quarter + digit2 * eighth, eighth), lanes(colour)]
        move = remote(spot, spot, ag_send.at[2, n], ag_recv.at[2, n], peer)
        move.start()
        stage.append(move)
    moves, stage = stage, []
    for n, (chunk, colour) in enumerate(items):
        moves[n].wait()
        (digit, peer), _ = orders(colour)
        spot = full.at[chunk, piece(core * half + digit * quarter, quarter), lanes(colour)]
        move = remote(spot, spot, ag_send.at[1, n], ag_recv.at[1, n], peer)
        move.start()
        stage.append(move)
    moves, stage = stage, []
    for n, (chunk, colour) in enumerate(items):
        moves[n].wait()
        spot = full.at[chunk, piece(core * half, half), lanes(colour)]
        move = remote(spot, spot, ag_send.at[0, n], ag_recv.at[0, n], core_peer)
        move.start()
        stage.append(move)
    finals = []
    for n, (chunk, colour) in enumerate(items):
        stage[n].wait()
        if colour == 2:
            final = pltpu.make_async_copy(full.at[chunk], grads_ref.at[chunk], fin_sem.at[chunk])
            final.start()
            finals.append(final)
    small_ref[...] = small[...]
    for move in out_moves:
        move.wait()
    pooled_ref[...] = pool[...]
    own_b.wait()
    own_i.wait()
    for final in finals:
        final.wait()


def finish_kernel(
    grads_ref, small_ref, pool_ref, bl_ref, ig_ref,
    block_ref, pooled_ref, igrad_ref, qkv_ref, qb_ref, vb_ref, out_ref, ob_ref, g1_ref, b1_ref,
    up_ref, ub_ref, down_ref, db_ref, g2_ref, b2_ref, sem,
):
    move1 = pltpu.make_async_copy(bl_ref, block_ref, sem.at[0])
    move2 = pltpu.make_async_copy(ig_ref, igrad_ref, sem.at[1])
    move1.start()
    move2.start()
    down_ref[...] = grads_ref[0].astype(F32)
    for i in range(4):
        up_ref[:, i * D : (i + 1) * D] = grads_ref[1, i * D : (i + 1) * D, :].astype(F32)
        ub_ref[:, i * D : (i + 1) * D] = small_ref[i : i + 1, :]
    out_ref[...] = grads_ref[2, :D, :].astype(F32)
    for i in range(3):
        qkv_ref[:, i * D : (i + 1) * D] = grads_ref[2, (i + 1) * D : (i + 2) * D, :].astype(F32)
    for m in range(4):
        pooled_ref[m] = pool_ref[m, :1, :]
    for row, ref in ((4, db_ref), (5, ob_ref), (6, qb_ref), (7, vb_ref), (8, g1_ref), (9, b1_ref), (10, g2_ref), (11, b2_ref)):
        ref[...] = small_ref[row : row + 1, :]
    move1.wait()
    move2.wait()


def body(
    ndp,
    inputs, lengths, cotangent, pool_cotangent, qkv_weight, query_bias, value_bias,
    out_weight, out_bias, norm1_gain, norm1_bias, up_weight, up_bias, down_weight,
    down_bias, norm2_gain, norm2_bias,
):
    any_spec = pl.BlockSpec(memory_space=pl.ANY)
    vmem = pl.BlockSpec(memory_space=pltpu.VMEM)
    smem = pl.BlockSpec(memory_space=pltpu.SMEM)
    extra = max(ndp.bit_length() - 4, 0)
    n_items = CHUNKS * 3

    def row(item):
        return item.reshape(1, -1)

    def v(*shape, dtype=BF16):
        return pltpu.VMEM(shape, dtype)

    dma = pltpu.SemaphoreType.DMA
    args = (
        inputs, lengths, cotangent, pool_cotangent,
        qkv_weight, row(query_bias), row(value_bias), out_weight, row(out_bias),
        row(norm1_gain), row(norm1_bias), up_weight, row(up_bias), down_weight, row(down_bias),
        row(norm2_gain), row(norm2_bias),
    )
    in_specs = [
        any_spec, smem, any_spec, vmem,
        any_spec, vmem, vmem, any_spec, vmem,
        vmem, vmem, any_spec, vmem, any_spec, vmem,
        vmem, vmem,
    ]
    results = pl.pallas_call(
        functools.partial(kernel, ndp),
        out_shape=(
            jax.ShapeDtypeStruct(inputs.shape, BF16),
            jax.ShapeDtypeStruct((4, 8, D), F32),
            jax.ShapeDtypeStruct(inputs.shape, BF16),
            jax.ShapeDtypeStruct((CHUNKS, ROWS, D), BF16),
            jax.ShapeDtypeStruct((16, D), F32),
        ),
        in_specs=in_specs,
        out_specs=(any_spec, vmem, any_spec, any_spec, vmem),
        scratch_shapes=[
            v(512, D), v(512, D), v(D, 3 * D), v(D, D), v(D, FF), v(FF, D), v(3 * D, D), v(D + 16, 512),
            v(D, 512), v(D, 512), v(D, 512), v(H * VROWS, 512), v(H, 512, 512), v(H, 8, 512, dtype=F32),
            v(D, 512), v(512, D, dtype=F32), v(512, 1, dtype=F32), v(512, D), v(512, FF), v(512, FF, dtype=F32),
            v(512, D, dtype=F32), v(512, D, dtype=F32), v(512, D), v(512, FF), v(512, D, dtype=F32),
            v(D, 512), v(3 * D, 512), v(512, D), v(512, D), v(4, 8, D, dtype=F32),
            v(CHUNKS, ROWS, D), v(CHUNKS, ROWS // 2, D), v(CHUNKS, ROWS // 4, D), v(CHUNKS, ROWS // 8, D),
            v(CHUNKS, 3 + extra, ROWS // 32, D),
            v(CHUNKS, ROWS // 2, D), v(CHUNKS, ROWS // 4, D), v(CHUNKS, ROWS // 8, D),
            v(CHUNKS, ROWS, D), v(16, D, dtype=F32), v(6 + extra, 16, D, dtype=F32),
            dma((4,)), dma((4,)), dma((2, 3)), dma((2, 3)), dma((2, 3)), dma((2, 3)), dma((3,)), dma((3,)),
            dma((6 + extra, n_items)), dma((6 + extra, n_items)), dma((6, n_items)), dma((6, n_items)),
            dma((6 + extra,)), dma((6 + extra,)), dma((CHUNKS,)),
        ],
        compiler_params=pltpu.CompilerParams(
            collective_id=0, has_side_effects=True, vmem_limit_bytes=58 * 2**20
        ),
    )(*args)
    block, pooled, igrad, grads, small = results

    def shape(*dims, dtype=F32):
        return jax.ShapeDtypeStruct(dims, dtype)

    outs = pl.pallas_call(
        finish_kernel,
        out_shape=(
            shape(*inputs.shape, dtype=BF16), shape(4, 1, D), shape(*inputs.shape, dtype=BF16),
            shape(D, 3 * D), shape(1, D), shape(1, D), shape(D, D), shape(1, D), shape(1, D), shape(1, D),
            shape(D, FF), shape(1, FF), shape(FF, D), shape(1, D), shape(1, D), shape(1, D),
        ),
        in_specs=[vmem, vmem, vmem, any_spec, any_spec],
        out_specs=(any_spec, vmem, any_spec) + (vmem,) * 13,
        scratch_shapes=[dma((2,))],
        compiler_params=pltpu.CompilerParams(vmem_limit_bytes=40 * 2**20),
    )(grads, small, pooled, block, igrad)
    outs = list(outs)
    for i in (4, 5, 7, 8, 9, 11, 13, 14, 15):
        outs[i] = outs[i].reshape(-1)
    return tuple(outs)


def solution(mesh):
    whole = P()
    return jax.shard_map(
        functools.partial(body, mesh.shape["dp"]),
        mesh=mesh,
        in_specs=(
            P(None, "dp", "seq", None), P(None, "dp"), P(None, "dp", "seq", None), P(None, "dp", None),
        ) + (whole,) * 13,
        out_specs=(
            P(None, "dp", "seq", None), P(None, "dp", None), P(None, "dp", "seq", None),
        ) + (whole,) * 13,
        check_vma=False,
    )
```

```python
import functools

import jax
import jax.numpy as jnp
from jax import lax
from jax.experimental import pallas as pl
from jax.experimental.pallas import tpu as pltpu
from jax.sharding import PartitionSpec as P

H = 12
HD = 32
D = 384
FF = 1536
EPS = 1e-6
F32 = jnp.float32
BF16 = jnp.bfloat16
MESH = pl.DeviceIdType.MESH
NN = (((1,), (0,)), ((), ()))
NT = (((1,), (1,)), ((), ()))
TN = (((0,), (0,)), ((), ()))
LOG2E = 1.4426950408889634
SCALE = HD**-0.5
VROWS = HD + 16
CHUNKS = 3
ROWS = 1536


def dot(left, right, dims):
    return lax.dot_general(left, right, dims, preferred_element_type=F32)


def gelu_and_slope(upper):
    cdf = 0.5 * (1.0 + lax.erf(upper * 2.0**-0.5))
    density = jnp.exp2((-0.5 * LOG2E) * (upper * upper)) * (2.0 * jnp.pi) ** -0.5
    return upper * cdf, cdf + upper * density


def layer_norm(values):
    centre = values - jnp.mean(values, axis=-1, keepdims=True)
    inverse = lax.rsqrt(jnp.mean(centre * centre, axis=-1, keepdims=True) + EPS)
    return centre * inverse, inverse


def norm_back(grad_out, normal, inverse, gain):
    scaled = grad_out * gain
    return inverse * (
        scaled
        - jnp.mean(scaled, axis=-1, keepdims=True)
        - normal * jnp.mean(scaled * normal, axis=-1, keepdims=True)
    )


def kernel(
    ndp,
    inputs_ref, lengths_ref, cot_ref, pool_ref,
    qkv_hbm, qb_ref, vb_ref, out_hbm, ob_ref, g1_ref, b1_ref,
    up_hbm, ub_ref, down_hbm, db_ref, g2_ref, b2_ref,
    block_ref, pooled_ref, igrad_ref, grads_ref, small_ref,
    x, cot, qkv_w, out_w, up_w, down_w, qkv_t, x_t,
    q_t, kd_t, kz_t, v_x, probs, inv, c_t, y1, r1, first_low, active, slope,
    lower, gsum, g_low, g_up, g_hid, gc_t, gj_t, bout, igr, pool,
    part, got0, got1, got2, got3, shard1, shard2, shard3, full, small, small_got, up_row,
    w_sem, loc_sem, in_send, in_recv, out_send, out_recv, pool_send, pool_recv,
    rs_send, rs_recv, ag_send, ag_recv, sm_send, sm_recv, fin_sem,
):
    dp = lax.axis_index("dp")
    sq = lax.axis_index("seq")
    core = lax.rem(sq, 2)
    yy = lax.div(sq, 2)
    xx = lax.rem(dp, 2)
    zz = lax.rem(lax.div(dp, 2), 4)
    extra = []
    bit = 8
    while bit < ndp:
        extra.append(bit)
        bit *= 2

    def flip(index, amount):
        digit = lax.rem(lax.div(index, amount), 2)
        return index + amount * (1 - 2 * digit)

    seq_peers = [lax.rem(sq + step, 4) for step in (1, 2, 3)]
    core_peer = (dp, flip(sq, 1))
    y_peer = (dp, flip(sq, 2))
    x_peer = (flip(dp, 1), sq)
    z_ids = [lax.rem(zz + step, 4) for step in (1, 2, 3)]
    z_peers = [(dp + 2 * (other - zz), sq) for other in z_ids]
    w_peers = [(flip(dp, amount), sq) for amount in extra]
    greeted = [(dp, peer) for peer in seq_peers] + [x_peer] + z_peers + w_peers

    loads = [
        pltpu.make_async_copy(src, dst, w_sem.at[i])
        for i, (src, dst) in enumerate(
            [(qkv_hbm, qkv_w), (out_hbm, out_w), (up_hbm, up_w), (down_hbm, down_w)]
        )
    ]
    for load in loads:
        load.start()
    own_rows = pl.ds(pl.multiple_of(sq * 128, 128), 128)
    own_x = pltpu.make_async_copy(inputs_ref.at[sq, 0], x.at[own_rows], loc_sem.at[0])
    own_c = pltpu.make_async_copy(cot_ref.at[sq, 0], cot.at[own_rows], loc_sem.at[1])
    own_x.start()
    own_c.start()

    barrier = pltpu.get_barrier_semaphore()
    for peer in greeted:
        pl.semaphore_signal(barrier, inc=1, device_id=peer, device_id_type=MESH)
    pl.semaphore_wait(barrier, len(greeted))

    def remote(src, dst, send, recv, peer):
        return pltpu.make_async_remote_copy(
            src_ref=src, dst_ref=dst, send_sem=send, recv_sem=recv,
            device_id=peer, device_id_type=MESH,
        )

    x_moves, c_moves = [], []
    for which, (src, dst, moves) in enumerate(((inputs_ref, x, x_moves), (cot_ref, cot, c_moves))):
        for i, peer in enumerate(seq_peers):
            move = remote(
                src.at[peer, 0], dst.at[own_rows],
                in_send.at[which, i], in_recv.at[which, i], (dp, peer),
            )
            move.start()
            moves.append(move)

    span = lengths_ref[0, sq]
    query_bias, value_bias, out_bias, gain_one, bias_one, up_bias, down_bias, gain_two, bias_two = (
        ref[...].reshape(1, -1)
        for ref in (qb_ref, vb_ref, ob_ref, g1_ref, b1_ref, ub_ref, db_ref, g2_ref, b2_ref)
    )
    up_row[...] = up_bias
    count = span.astype(F32)
    lane_valid = lax.broadcasted_iota(jnp.int32, (1, 512), 1) < span

    loads[0].wait()

    def turn(i, carry):
        cols = pl.ds(pl.multiple_of(i * 128, 128), 128)
        qkv_t[cols, :] = qkv_w[:, cols].T
        return carry

    lax.fori_loop(0, 9, turn, 0)
    own_x.wait()
    for move in x_moves:
        move.wait()

    x_t[:D, :] = x[...].T
    x_t[D:, :] = jnp.ones((16, 512), BF16)

    qcol = jnp.broadcast_to(query_bias, (8, D)).T[:, :1]
    vcol = jnp.broadcast_to(value_bias, (8, D)).T[:, :1]
    q_t[...] = (dot(qkv_t[:D, :], x[...], NT) + qcol).astype(BF16)
    keys = dot(qkv_t[D : 2 * D, :], x[...], NT)
    kd_t[...] = jnp.where(lane_valid, keys, keys[:, :1]).astype(BF16)
    kz_t[...] = jnp.where(lane_valid, keys, 0.0).astype(BF16)
    values = jnp.where(lane_valid, dot(qkv_t[2 * D :, :], x[...], NT) + vcol, 0.0).astype(BF16)
    ones_row = jnp.broadcast_to(jnp.where(lane_valid, 1.0, 0.0), (16, 512)).astype(BF16)
    for h in range(H):
        v_x[h * VROWS : h * VROWS + HD, :] = values[h * HD : (h + 1) * HD, :]
        v_x[h * VROWS + HD : (h + 1) * VROWS, :] = ones_row

    def attend(h, carry):
        rows = pl.ds(pl.multiple_of(h * HD, HD), HD)
        scores = dot(kd_t[rows, :], q_t[rows, :], TN)
        peak = jnp.max(scores, axis=0, keepdims=True)
        raised = jnp.exp2(scores * (SCALE * LOG2E) - peak * (SCALE * LOG2E)).astype(BF16)
        probs[h] = raised
        both = dot(v_x[pl.ds(pl.multiple_of(h * VROWS, 16), VROWS), :], raised, NN)
        inverse = 1.0 / both[HD : HD + 1, :]
        inv[h] = jnp.broadcast_to(inverse, (8, 512))
        c_t[rows, :] = (both[:HD, :] * inverse).astype(BF16)
        return carry

    lax.fori_loop(0, H, attend, 0)

    loads[1].wait()

    def rows_of(i, size):
        return pl.ds(pl.multiple_of(i * size, size), size)

    lower[...] = dot(c_t[...], out_w[...], TN)

    def norm_one(i, carry):
        rows = rows_of(i, 128)
        normal, inverse = layer_norm(x[rows, :].astype(F32) + lower[rows, :] + out_bias)
        y1[rows, :] = normal
        r1[rows, :] = inverse
        first_low[rows, :] = (normal * gain_one + bias_one).astype(BF16)
        return carry

    lax.fori_loop(0, 4, norm_one, 0)
    loads[2].wait()

    def raise_up(i, carry):
        cols = rows_of(i, 256)
        upper = dot(first_low[...], up_w[:, cols], NN) + up_row[:, cols]
        act, slp = gelu_and_slope(upper)
        active[:, cols] = act.astype(BF16)
        slope[:, cols] = slp
        return carry

    lax.fori_loop(0, FF // 256, raise_up, 0)
    loads[3].wait()
    lower[...] = dot(active[...], down_w[...], NN)
    own_c.wait()
    for move in c_moves:
        move.wait()
    chosen = lax.broadcasted_iota(jnp.int32, (4, D), 0) == sq
    pool_share = jnp.sum(jnp.where(chosen, pool_ref[0].astype(F32), 0.0), axis=0, keepdims=True) / count

    zero_row = jnp.zeros((1, D), F32)

    def norm_two(i, carry):
        sums, gain_sum, bias_sum, down_sum = carry
        rows = rows_of(i, 128)
        firsts = y1[rows, :] * gain_one + bias_one
        normal, inverse = layer_norm(firsts + lower[rows, :] + down_bias)
        here = lax.broadcasted_iota(jnp.int32, (128, 1), 0) + i * 128 < span
        masked = jnp.where(here, normal * gain_two + bias_two, 0.0)
        bout[rows, :] = masked.astype(BF16)
        grad = jnp.where(here, cot[rows, :].astype(F32) + pool_share, 0.0)
        grad_in = norm_back(grad, normal, inverse, gain_two)
        gsum[rows, :] = grad_in
        low = grad_in.astype(BF16)
        g_low[rows, :] = low
        return (
            sums + jnp.sum(masked, axis=0, keepdims=True),
            gain_sum + jnp.sum(grad * normal, axis=0, keepdims=True),
            bias_sum + jnp.sum(grad, axis=0, keepdims=True),
            down_sum + jnp.sum(low.astype(F32), axis=0, keepdims=True),
        )

    sums, gain2, bias2, down_sum = lax.fori_loop(
        0, 4, norm_two, (zero_row, zero_row, zero_row, zero_row)
    )
    pool[sq] = jnp.broadcast_to(sums / count, (8, D))
    small[4:5, :] = down_sum
    small[10:11, :] = gain2
    small[11:12, :] = bias2

    out_moves = []
    for i, peer in enumerate(seq_peers):
        move = remote(
            bout.at[pl.ds(pl.multiple_of(peer * 128, 128), 128)], block_ref.at[sq, 0],
            out_send.at[0, i], out_recv.at[0, i], (dp, peer),
        )
        move.start()
        out_moves.append(move)
        move = remote(pool.at[sq], pool.at[sq], pool_send.at[i], pool_recv.at[i], (dp, peer))
        move.start()
        out_moves.append(move)
    own_b = pltpu.make_async_copy(bout.at[own_rows], block_ref.at[sq, 0], loc_sem.at[2])
    own_b.start()

    part[0] = dot(active[...], g_low[...], TN).astype(BF16)

    def back_up(i, carry):
        cols = rows_of(i, 256)
        low = (dot(g_low[...], down_w[cols, :], NT) * slope[:, cols]).astype(BF16)
        g_up[:, cols] = low
        return carry

    lax.fori_loop(0, FF // 256, back_up, 0)
    for i in range(4):
        small[i : i + 1, :] = jnp.sum(
            g_up[:, i * D : (i + 1) * D].astype(F32), axis=0, keepdims=True
        )
        part[1, i * D : (i + 1) * D, :] = dot(
            first_low[...], g_up[:, i * D : (i + 1) * D], TN
        ).astype(BF16)
    lower[...] = dot(g_up[...], up_w[...], NT)

    def norm_one_back(i, carry):
        gain_sum, bias_sum, out_sum = carry
        rows = rows_of(i, 128)
        grad = gsum[rows, :] + lower[rows, :]
        normal = y1[rows, :]
        grad_in = norm_back(grad, normal, r1[rows, :], gain_one)
        g_hid[rows, :] = grad_in
        low = grad_in.astype(BF16)
        g_low[rows, :] = low
        return (
            gain_sum + jnp.sum(grad * normal, axis=0, keepdims=True),
            bias_sum + jnp.sum(grad, axis=0, keepdims=True),
            out_sum + jnp.sum(low.astype(F32), axis=0, keepdims=True),
        )

    gain1, bias1, out_sum = lax.fori_loop(0, 4, norm_one_back, (zero_row, zero_row, zero_row))
    small[5:6, :] = out_sum
    small[8:9, :] = gain1
    small[9:10, :] = bias1
    small[12:16, :] = jnp.zeros((4, D), F32)

    part[2, :D, :] = dot(c_t[...], g_low[...], NN).astype(BF16)
    gc_t[...] = dot(out_w[...], g_low[...], NT).astype(BF16)

    def attend_back(h, carry):
        rows = pl.ds(pl.multiple_of(h * HD, HD), HD)
        inverse = inv[h][:1, :]
        grad_c = (gc_t[rows, :].astype(F32) * inverse).astype(BF16)
        inner = jnp.sum(grad_c.astype(F32) * c_t[rows, :].astype(F32), axis=0, keepdims=True)
        grad_w = dot(v_x[pl.ds(pl.multiple_of(h * VROWS, 16), HD), :], grad_c, TN)
        weights = probs[h]
        grad_s = (weights.astype(F32) * (grad_w - inner)).astype(BF16)
        gj_t[rows, :] = (dot(kz_t[rows, :], grad_s, NN) * SCALE).astype(BF16)
        gk = jnp.where(lane_valid, dot(q_t[rows, :], grad_s, NT) * SCALE, 0.0)
        gj_t[pl.ds(pl.multiple_of(D + h * HD, HD), HD), :] = gk.astype(BF16)
        gv = jnp.where(lane_valid, dot(grad_c, weights, NT), 0.0)
        gj_t[pl.ds(pl.multiple_of(2 * D + h * HD, HD), HD), :] = gv.astype(BF16)
        return carry

    lax.fori_loop(0, H, attend_back, 0)

    for j in range(3):
        both = dot(x_t[...], gj_t[j * D : (j + 1) * D, :], NT)
        part[2, (j + 1) * D : (j + 2) * D, :] = both[:D, :].astype(BF16)
        if j == 0:
            small[6:7, :] = both[D : D + 1, :]
        if j == 2:
            small[7:8, :] = both[D : D + 1, :]
    igr[...] = (g_hid[...] + dot(gj_t[...], qkv_t[...], TN)).astype(BF16)
    for i, peer in enumerate(seq_peers):
        move = remote(
            igr.at[pl.ds(pl.multiple_of(peer * 128, 128), 128)], igrad_ref.at[sq, 0],
            out_send.at[1, i], out_recv.at[1, i], (dp, peer),
        )
        move.start()
        out_moves.append(move)
    own_i = pltpu.make_async_copy(igr.at[own_rows], igrad_ref.at[sq, 0], loc_sem.at[3])
    own_i.start()

    items = [(chunk, colour) for chunk in range(CHUNKS) for colour in range(3)]

    def lanes(colour):
        return pl.ds(colour * 128, 128)

    def piece(base, size):
        return pl.ds(pl.multiple_of(base, 16), size)

    half, quarter, eighth, unit = ROWS // 2, ROWS // 4, ROWS // 8, ROWS // 32

    def orders(colour):
        if colour == 0:
            return (yy, y_peer), (xx, x_peer)
        return (xx, x_peer), (yy, y_peer)

    def small_step(step, peer):
        move = remote(small, small_got.at[step], sm_send.at[step], sm_recv.at[step], peer)
        move.start()
        move.wait()
        small[...] = small[...] + small_got[step]

    moves = []
    for n, (chunk, colour) in enumerate(items):
        move = remote(
            part.at[chunk, piece((1 - core) * half, half), lanes(colour)],
            got0.at[chunk, :, lanes(colour)], rs_send.at[0, n], rs_recv.at[0, n], core_peer,
        )
        move.start()
        moves.append(move)
    small_step(0, core_peer)
    stage = []
    for n, (chunk, colour) in enumerate(items):
        moves[n].wait()
        shard1[chunk, :, lanes(colour)] = (
            part[chunk, piece(core * half, half), lanes(colour)].astype(F32)
            + got0[chunk, :, lanes(colour)].astype(F32)
        ).astype(BF16)
        (digit, peer), _ = orders(colour)
        move = remote(
            shard1.at[chunk, piece((1 - digit) * quarter, quarter), lanes(colour)],
            got1.at[chunk, :, lanes(colour)], rs_send.at[1, n], rs_recv.at[1, n], peer,
        )
        move.start()
        stage.append(move)
    small_step(1, y_peer)
    moves, stage = stage, []
    for n, (chunk, colour) in enumerate(items):
        moves[n].wait()
        (digit, _), (digit2, peer) = orders(colour)
        shard2[chunk, :, lanes(colour)] = (
            shard1[chunk, piece(digit * quarter, quarter), lanes(colour)].astype(F32)
            + got1[chunk, :, lanes(colour)].astype(F32)
        ).astype(BF16)
        move = remote(
            shard2.at[chunk, piece((1 - digit2) * eighth, eighth), lanes(colour)],
            got2.at[chunk, :, lanes(colour)], rs_send.at[2, n], rs_recv.at[2, n], peer,
        )
        move.start()
        stage.append(move)
    small_step(2, x_peer)
    moves, stage = stage, []
    for n, (chunk, colour) in enumerate(items):
        moves[n].wait()
        _, (digit2, _) = orders(colour)
        shard3[chunk, :, lanes(colour)] = (
            shard2[chunk, piece(digit2 * eighth, eighth), lanes(colour)].astype(F32)
            + got2[chunk, :, lanes(colour)].astype(F32)
        ).astype(BF16)
        for j in range(3):
            move = remote(
                shard3.at[chunk, piece(z_ids[j] * unit, unit), lanes(colour)],
                got3.at[chunk, j, :, lanes(colour)],
                rs_send.at[3 + j, n], rs_recv.at[3 + j, n], z_peers[j],
            )
            move.start()
            stage.append(move)
    z_moves = []
    for j in range(3):
        move = remote(small, small_got.at[3 + j], sm_send.at[3 + j], sm_recv.at[3 + j], z_peers[j])
        move.start()
        z_moves.append(move)
    for move in z_moves:
        move.wait()
    parts4 = [small[...]] + [small_got[3 + j] for j in range(3)]

    def by_place(place):
        total = None
        for j in range(4):
            term = jnp.where(lax.rem(zz - j + 4, 4) == place, parts4[j], 0.0)
            total = term if total is None else total + term
        return total

    small[...] = (by_place(0) + by_place(1)) + (by_place(2) + by_place(3))
    for e, peer in enumerate(w_peers):
        small_step(6 + e, peer)

    moves, stage = stage, []
    for n, (chunk, colour) in enumerate(items):
        total = shard3[chunk, piece(zz * unit, unit), lanes(colour)].astype(F32)
        for j in range(3):
            moves[3 * n + j].wait()
            total = total + got3[chunk, j, :, lanes(colour)].astype(F32)
        (digit, _), (digit2, _) = orders(colour)
        base = core * half + digit * quarter + digit2 * eighth
        mine = piece(base + zz * unit, unit)
        full[chunk, mine, lanes(colour)] = total.astype(BF16)
        for e, peer in enumerate(w_peers):
            move = remote(
                full.at[chunk, mine, lanes(colour)],
                got3.at[chunk, 3 + e, :, lanes(colour)],
                rs_send.at[6 + e, n], rs_recv.at[6 + e, n], peer,
            )
            move.start()
            move.wait()
            full[chunk, mine, lanes(colour)] = (
                full[chunk, mine, lanes(colour)].astype(F32)
                + got3[chunk, 3 + e, :, lanes(colour)].astype(F32)
            ).astype(BF16)
        for j in range(3):
            spot = full.at[chunk, mine, lanes(colour)]
            move = remote(spot, spot, ag_send.at[3 + j, n], ag_recv.at[3 + j, n], z_peers[j])
            move.start()
            stage.append(move)
    moves, stage = stage, []
    for n, (chunk, colour) in enumerate(items):
        for j in range(3):
            moves[3 * n + j].wait()
        (digit, _), (digit2, peer) = orders(colour)
        spot = full.at[chunk, piece(core * half + digit * quarter + digit2 * eighth, eighth), lanes(colour)]
        move = remote(spot, spot, ag_send.at[2, n], ag_recv.at[2, n], peer)
        move.start()
        stage.append(move)
    moves, stage = stage, []
    for n, (chunk, colour) in enumerate(items):
        moves[n].wait()
        (digit, peer), _ = orders(colour)
        spot = full.at[chunk, piece(core * half + digit * quarter, quarter), lanes(colour)]
        move = remote(spot, spot, ag_send.at[1, n], ag_recv.at[1, n], peer)
        move.start()
        stage.append(move)
    moves, stage = stage, []
    for n, (chunk, colour) in enumerate(items):
        moves[n].wait()
        spot = full.at[chunk, piece(core * half, half), lanes(colour)]
        move = remote(spot, spot, ag_send.at[0, n], ag_recv.at[0, n], core_peer)
        move.start()
        stage.append(move)
    finals = []
    for n, (chunk, colour) in enumerate(items):
        stage[n].wait()
        if colour == 2:
            final = pltpu.make_async_copy(full.at[chunk], grads_ref.at[chunk], fin_sem.at[chunk])
            final.start()
            finals.append(final)
    small_ref[...] = small[...]
    for move in out_moves:
        move.wait()
    pooled_ref[...] = pool[...]
    own_b.wait()
    own_i.wait()
    for final in finals:
        final.wait()


def finish_kernel(
    grads_ref, small_ref, pool_ref, bl_ref, ig_ref,
    block_ref, pooled_ref, igrad_ref, qkv_ref, qb_ref, vb_ref, out_ref, ob_ref, g1_ref, b1_ref,
    up_ref, ub_ref, down_ref, db_ref, g2_ref, b2_ref,
    low, wide, held, in_sem, out_sem, sem,
):
    moves, loads = [], []
    for i in range(12):
        load = pltpu.make_async_copy(
            grads_ref.at[i // 4, pl.ds((i % 4) * D, D)], low.at[i], in_sem.at[i]
        )
        load.start()
        loads.append(load)
    passes = ((bl_ref, block_ref), (ig_ref, igrad_ref))
    for i, (src, _) in enumerate(passes):
        load = pltpu.make_async_copy(src, held.at[i], sem.at[i])
        load.start()
        loads.append(load)
    for i in range(4):
        ub_ref[i * D : (i + 1) * D] = small_ref[i, :]
    for m in range(4):
        pooled_ref[m] = pool_ref[m, :1, :]
    for row, ref in ((4, db_ref), (5, ob_ref), (6, qb_ref), (7, vb_ref), (8, g1_ref), (9, b1_ref), (10, g2_ref), (11, b2_ref)):
        ref[...] = small_ref[row, :]
    for i in range(12):
        loads[i].wait()
        wide[i] = low[i].astype(F32)
        span = pl.ds((i % 4) * D, D)
        if i < 4:
            place = down_ref.at[span]
        elif i < 8:
            place = up_ref.at[:, span]
        elif i == 8:
            place = out_ref
        else:
            place = qkv_ref.at[:, pl.ds((i - 9) * D, D)]
        move = pltpu.make_async_copy(wide.at[i], place, out_sem.at[i])
        move.start()
        moves.append(move)
    for i, (_, dst) in enumerate(passes):
        loads[12 + i].wait()
        move = pltpu.make_async_copy(held.at[i], dst, sem.at[2 + i])
        move.start()
        moves.append(move)
    for move in moves:
        move.wait()


def body(
    ndp,
    inputs, lengths, cotangent, pool_cotangent, qkv_weight, query_bias, value_bias,
    out_weight, out_bias, norm1_gain, norm1_bias, up_weight, up_bias, down_weight,
    down_bias, norm2_gain, norm2_bias,
):
    any_spec = pl.BlockSpec(memory_space=pltpu.HBM)
    vmem = pl.BlockSpec(memory_space=pltpu.VMEM)
    smem = pl.BlockSpec(memory_space=pltpu.SMEM)
    extra = max(ndp.bit_length() - 4, 0)
    n_items = CHUNKS * 3

    def v(*shape, dtype=BF16):
        return pltpu.VMEM(shape, dtype)

    dma = pltpu.SemaphoreType.DMA
    args = (
        inputs, lengths.T, cotangent, jnp.transpose(pool_cotangent, (1, 0, 2)),
        qkv_weight, query_bias, value_bias, out_weight, out_bias,
        norm1_gain, norm1_bias, up_weight, up_bias, down_weight, down_bias,
        norm2_gain, norm2_bias,
    )
    in_specs = [
        any_spec, smem, any_spec, vmem,
        any_spec, vmem, vmem, any_spec, vmem,
        vmem, vmem, any_spec, vmem, any_spec, vmem,
        vmem, vmem,
    ]
    results = pl.pallas_call(
        functools.partial(kernel, ndp),
        out_shape=(
            jax.ShapeDtypeStruct(inputs.shape, BF16),
            jax.ShapeDtypeStruct((4, 8, D), F32),
            jax.ShapeDtypeStruct(inputs.shape, BF16),
            jax.ShapeDtypeStruct((CHUNKS, ROWS, D), BF16),
            jax.ShapeDtypeStruct((16, D), F32),
        ),
        in_specs=in_specs,
        out_specs=(any_spec, vmem, any_spec, any_spec, vmem),
        scratch_shapes=[
            v(512, D), v(512, D), v(D, 3 * D), v(D, D), v(D, FF), v(FF, D), v(3 * D, D), v(D + 16, 512),
            v(D, 512), v(D, 512), v(D, 512), v(H * VROWS, 512), v(H, 512, 512), v(H, 8, 512, dtype=F32),
            v(D, 512), v(512, D, dtype=F32), v(512, 1, dtype=F32), v(512, D), v(512, FF), v(512, FF, dtype=F32),
            v(512, D, dtype=F32), v(512, D, dtype=F32), v(512, D), v(512, FF), v(512, D, dtype=F32),
            v(D, 512), v(3 * D, 512), v(512, D), v(512, D), v(4, 8, D, dtype=F32),
            v(CHUNKS, ROWS, D), v(CHUNKS, ROWS // 2, D), v(CHUNKS, ROWS // 4, D), v(CHUNKS, ROWS // 8, D),
            v(CHUNKS, 3 + extra, ROWS // 32, D),
            v(CHUNKS, ROWS // 2, D), v(CHUNKS, ROWS // 4, D), v(CHUNKS, ROWS // 8, D),
            v(CHUNKS, ROWS, D), v(16, D, dtype=F32), v(6 + extra, 16, D, dtype=F32), v(1, FF, dtype=F32),
            dma((4,)), dma((4,)), dma((2, 3)), dma((2, 3)), dma((2, 3)), dma((2, 3)), dma((3,)), dma((3,)),
            dma((6 + extra, n_items)), dma((6 + extra, n_items)), dma((6, n_items)), dma((6, n_items)),
            dma((6 + extra,)), dma((6 + extra,)), dma((CHUNKS,)),
        ],
        compiler_params=pltpu.CompilerParams(
            collective_id=0, has_side_effects=True, vmem_limit_bytes=58 * 2**20
        ),
    )(*args)
    block, pooled, igrad, grads, small = results

    def shape(*dims, dtype=F32):
        return jax.ShapeDtypeStruct(dims, dtype)

    outs = pl.pallas_call(
        finish_kernel,
        out_shape=(
            shape(*inputs.shape, dtype=BF16), shape(4, 1, D), shape(*inputs.shape, dtype=BF16),
            shape(D, 3 * D), shape(D), shape(D), shape(D, D), shape(D), shape(D), shape(D),
            shape(D, FF), shape(FF), shape(FF, D), shape(D), shape(D), shape(D),
        ),
        in_specs=[any_spec, vmem, vmem, any_spec, any_spec],
        out_specs=(
            any_spec, vmem, any_spec, any_spec, vmem, vmem, any_spec, vmem, vmem, vmem,
            any_spec, vmem, any_spec, vmem, vmem, vmem,
        ),
        scratch_shapes=[v(12, D, D), v(12, D, D, dtype=F32), v(2, *inputs.shape), dma((12,)), dma((12,)), dma((4,))],
        compiler_params=pltpu.CompilerParams(vmem_limit_bytes=58 * 2**20),
    )(grads, small, pooled, block, igrad)
    return outs


def solution(mesh):
    whole = P()
    return jax.shard_map(
        functools.partial(body, mesh.shape["dp"]),
        mesh=mesh,
        in_specs=(
            P(None, "dp", "seq", None), P(None, "dp"), P(None, "dp", "seq", None), P(None, "dp", None),
        ) + (whole,) * 13,
        out_specs=(
            P(None, "dp", "seq", None), P(None, "dp", None), P(None, "dp", "seq", None),
        ) + (whole,) * 13,
        check_vma=False,
    )
```

```python
import functools

import jax
import jax.numpy as jnp
from jax import lax
from jax.experimental import pallas as pl
from jax.experimental.pallas import tpu as pltpu
from jax.sharding import PartitionSpec as P

H = 12
HD = 32
D = 384
FF = 1536
EPS = 1e-6
F32 = jnp.float32
BF16 = jnp.bfloat16
MESH = pl.DeviceIdType.MESH
NN = (((1,), (0,)), ((), ()))
NT = (((1,), (1,)), ((), ()))
TN = (((0,), (0,)), ((), ()))
LOG2E = 1.4426950408889634
SCALE = HD**-0.5
VROWS = HD + 16
CHUNKS = 3
ROWS = 1536
GROUPS = 3
ORDERS = (
    ("x", "y", "z1", "z2"), ("y", "x", "z1", "z2"), ("z1", "z2", "x", "y"),
    ("x", "y", "z1", "z2"), ("y", "x", "z1", "z2"), ("z1", "z2", "x", "y"),
)
HALVE_TIMES = (0.0, 1.5, 5.5, 8.5, 11.0, 13.5, 16.0, 18.5, 21.0, 24.5, 25.5)
SPREAD_TIMES = (0.0, 1.2, 5.5, 10.5, 14.5, 16.5)
VECTOR_TIMES = (0.0, 1.2, 4.0, 6.8, 10.5)


def dot(left, right, dims):
    return lax.dot_general(left, right, dims, preferred_element_type=F32)


def gelu_and_slope(upper):
    cdf = 0.5 * (1.0 + lax.erf(upper * 2.0**-0.5))
    density = jnp.exp2((-0.5 * LOG2E) * (upper * upper)) * (2.0 * jnp.pi) ** -0.5
    return upper * cdf, cdf + upper * density


def layer_norm(values):
    centre = values - jnp.mean(values, axis=-1, keepdims=True)
    inverse = lax.rsqrt(jnp.mean(centre * centre, axis=-1, keepdims=True) + EPS)
    return centre * inverse, inverse


def norm_back(grad_out, normal, inverse, gain):
    scaled = grad_out * gain
    return inverse * (
        scaled
        - jnp.mean(scaled, axis=-1, keepdims=True)
        - normal * jnp.mean(scaled * normal, axis=-1, keepdims=True)
    )


def kernel(
    ndp,
    inputs_ref, lengths_ref, cot_ref, pool_ref,
    qkv_hbm, qb_ref, vb_ref, out_hbm, ob_ref, g1_ref, b1_ref,
    up_hbm, ub_ref, down_hbm, db_ref, g2_ref, b2_ref,
    block_ref, pooled_ref, igrad_ref, full, small_ref,
    x, cot, qkv_w, out_w, up_w, down_w, qkv_t, x_t,
    q_t, kd_t, kz_t, v_x, probs, inv, c_t, y1, r1, first_low, active, slope,
    lower, gsum, g_low, g_up, g_hid, gc_t, gj_t, bout, igr, pool,
    part, got0, got1, got2, got3, got4, sum0, sum1, sum2, sum3, blk0, blk1, blk2, blk_sum,
    small, small_got, small_z, up_row,
    w_sem, loc_sem, in_send, in_recv, out_send, out_recv, pool_send, pool_recv,
    rs_send, rs_recv, ag_send, ag_recv, blk_send, blk_recv, sm_send, sm_recv,
):
    dp = lax.axis_index("dp")
    sq = lax.axis_index("seq")
    core = lax.rem(sq, 2)
    yy = lax.div(sq, 2)
    xx = lax.rem(dp, 2)
    zz = lax.rem(lax.div(dp, 2), 4)
    extra = []
    bit = 8
    while bit < ndp:
        extra.append(bit)
        bit *= 2

    def flip(index, amount):
        digit = lax.rem(lax.div(index, amount), 2)
        return index + amount * (1 - 2 * digit)

    seq_peers = [lax.rem(sq + step, 4) for step in (1, 2, 3)]
    core_peer = (dp, flip(sq, 1))
    y_peer = (dp, flip(sq, 2))
    x_peer = (flip(dp, 1), sq)
    xy_peer = (flip(dp, 1), flip(sq, 2))
    z_peers = [(dp + 2 * (lax.rem(zz + step, 4) - zz), sq) for step in (1, 2, 3)]
    w_peers = [(flip(dp, amount), sq) for amount in extra]
    greeted = [(dp, peer) for peer in seq_peers] + [x_peer, xy_peer] + z_peers + w_peers
    halvings = {
        "core": (core, core_peer),
        "y": (yy, y_peer),
        "x": (xx, x_peer),
        "z1": (lax.rem(zz, 2), (flip(dp, 2), sq)),
        "z2": (lax.div(zz, 2), (flip(dp, 4), sq)),
    }

    loads = [
        pltpu.make_async_copy(src, dst, w_sem.at[i])
        for i, (src, dst) in enumerate(
            [(qkv_hbm, qkv_w), (out_hbm, out_w), (up_hbm, up_w), (down_hbm, down_w)]
        )
    ]
    for load in loads:
        load.start()
    own_rows = pl.ds(pl.multiple_of(sq * 128, 128), 128)
    own_x = pltpu.make_async_copy(inputs_ref.at[sq, 0], x.at[own_rows], loc_sem.at[0])
    own_c = pltpu.make_async_copy(cot_ref.at[sq, 0], cot.at[own_rows], loc_sem.at[1])
    own_x.start()
    own_c.start()

    barrier = pltpu.get_barrier_semaphore()
    for peer in greeted:
        pl.semaphore_signal(barrier, inc=1, device_id=peer, device_id_type=MESH)
    pl.semaphore_wait(barrier, len(greeted))

    def remote(src, dst, send, recv, peer):
        return pltpu.make_async_remote_copy(
            src_ref=src, dst_ref=dst, send_sem=send, recv_sem=recv,
            device_id=peer, device_id_type=MESH,
        )

    x_moves, c_moves = [], []
    for which, (src, dst, moves) in enumerate(((inputs_ref, x, x_moves), (cot_ref, cot, c_moves))):
        for i, peer in enumerate(seq_peers):
            move = remote(
                src.at[peer, 0], dst.at[own_rows],
                in_send.at[which, i], in_recv.at[which, i], (dp, peer),
            )
            moves.append(move)
    for move in x_moves:
        move.start()

    span = lengths_ref[0, sq]
    query_bias, value_bias, out_bias, gain_one, bias_one, up_bias, down_bias, gain_two, bias_two = (
        ref[...].reshape(1, -1)
        for ref in (qb_ref, vb_ref, ob_ref, g1_ref, b1_ref, ub_ref, db_ref, g2_ref, b2_ref)
    )
    up_row[...] = up_bias
    count = span.astype(F32)
    lane_valid = lax.broadcasted_iota(jnp.int32, (1, 512), 1) < span

    loads[0].wait()

    for i in range(3):
        for g in range(GROUPS):
            qkv_t[g * D + i * 128 : g * D + (i + 1) * 128, :] = qkv_w[:, i * D + g * 128 : i * D + (g + 1) * 128].T
    own_x.wait()
    for move in x_moves:
        move.wait()
    for move in c_moves:
        move.start()

    x_t[:D, :] = x[...].T
    x_t[D:, :] = jnp.ones((16, 512), BF16)

    qcol = jnp.broadcast_to(query_bias, (8, D)).T[:, :1]
    vcol = jnp.broadcast_to(value_bias, (8, D)).T[:, :1]
    ones_row = jnp.broadcast_to(jnp.where(lane_valid, 1.0, 0.0), (16, 512)).astype(BF16)
    for g in range(GROUPS):
        feats = slice(g * 128, (g + 1) * 128)
        joined = dot(qkv_t[g * D : (g + 1) * D, :], x[...], NT)
        q_t[feats, :] = (joined[:128] + qcol[feats]).astype(BF16)
        keys = joined[128:256]
        kd_t[feats, :] = jnp.where(lane_valid, keys, keys[:, :1]).astype(BF16)
        kz_t[feats, :] = jnp.where(lane_valid, keys, 0.0).astype(BF16)
        values = jnp.where(lane_valid, joined[256:] + vcol[feats], 0.0).astype(BF16)
        for i in range(4):
            h = 4 * g + i
            v_x[h * VROWS : h * VROWS + HD, :] = values[i * HD : (i + 1) * HD, :]
            v_x[h * VROWS + HD : (h + 1) * VROWS, :] = ones_row

    def attend(h, carry):
        rows = pl.ds(pl.multiple_of(h * HD, HD), HD)
        scores = dot(kd_t[rows, :], q_t[rows, :], TN)
        peak = jnp.max(scores, axis=0, keepdims=True)
        raised = jnp.exp2(scores * (SCALE * LOG2E) - peak * (SCALE * LOG2E)).astype(BF16)
        probs[h] = raised
        both = dot(v_x[pl.ds(pl.multiple_of(h * VROWS, 16), VROWS), :], raised, NN)
        inverse = 1.0 / both[HD : HD + 1, :]
        inv[h] = jnp.broadcast_to(inverse, (8, 512))
        c_t[rows, :] = (both[:HD, :] * inverse).astype(BF16)
        return carry

    lax.fori_loop(0, H, attend, 0, unroll=4)

    loads[1].wait()

    def rows_of(i, size):
        return pl.ds(pl.multiple_of(i * size, size), size)

    lower[...] = dot(c_t[...], out_w[...], TN)

    def norm_one(i, carry):
        rows = rows_of(i, 128)
        normal, inverse = layer_norm(x[rows, :].astype(F32) + lower[rows, :] + out_bias)
        y1[rows, :] = normal
        r1[rows, :] = inverse
        first_low[rows, :] = (normal * gain_one + bias_one).astype(BF16)
        return carry

    lax.fori_loop(0, 4, norm_one, 0)
    loads[2].wait()

    def raise_up(i, carry):
        cols = rows_of(i, 256)
        upper = dot(first_low[...], up_w[:, cols], NN) + up_row[:, cols]
        act, slp = gelu_and_slope(upper)
        active[:, cols] = act.astype(BF16)
        slope[:, cols] = slp
        return carry

    lax.fori_loop(0, FF // 256, raise_up, 0)
    loads[3].wait()
    lower[...] = dot(active[...], down_w[...], NN)
    own_c.wait()
    for move in c_moves:
        move.wait()
    chosen = lax.broadcasted_iota(jnp.int32, (4, D), 0) == sq
    pool_share = jnp.sum(jnp.where(chosen, pool_ref[0].astype(F32), 0.0), axis=0, keepdims=True) / count

    zero_row = jnp.zeros((1, D), F32)

    def norm_two(i, carry):
        sums, gain_sum, bias_sum, down_sum = carry
        rows = rows_of(i, 128)
        firsts = y1[rows, :] * gain_one + bias_one
        normal, inverse = layer_norm(firsts + lower[rows, :] + down_bias)
        here = lax.broadcasted_iota(jnp.int32, (128, 1), 0) + i * 128 < span
        masked = jnp.where(here, normal * gain_two + bias_two, 0.0)
        bout[rows, :] = masked.astype(BF16)
        grad = jnp.where(here, cot[rows, :].astype(F32) + pool_share, 0.0)
        grad_in = norm_back(grad, normal, inverse, gain_two)
        gsum[rows, :] = grad_in
        low = grad_in.astype(BF16)
        g_low[rows, :] = low
        return (
            sums + jnp.sum(masked, axis=0, keepdims=True),
            gain_sum + jnp.sum(grad * normal, axis=0, keepdims=True),
            bias_sum + jnp.sum(grad, axis=0, keepdims=True),
            down_sum + jnp.sum(low.astype(F32), axis=0, keepdims=True),
        )

    sums, gain2, bias2, down_sum = lax.fori_loop(
        0, 4, norm_two, (zero_row, zero_row, zero_row, zero_row)
    )
    pool[sq] = jnp.broadcast_to(sums / count, (8, D))
    small[4:5, :] = down_sum
    small[10:11, :] = gain2
    small[11:12, :] = bias2

    out_moves = []
    for i, peer in enumerate(seq_peers):
        move = remote(
            bout.at[pl.ds(pl.multiple_of(peer * 128, 128), 128)], block_ref.at[sq, 0],
            out_send.at[0, i], out_recv.at[0, i], (dp, peer),
        )
        move.start()
        out_moves.append(move)
        move = remote(pool.at[sq], pool.at[sq], pool_send.at[i], pool_recv.at[i], (dp, peer))
        move.start()
        out_moves.append(move)
    own_b = pltpu.make_async_copy(bout.at[own_rows], block_ref.at[sq, 0], loc_sem.at[2])
    own_b.start()

    def add(left, right):
        return (left.astype(F32) + right.astype(F32)).astype(BF16)

    def piece(base, size):
        return pl.ds(pl.multiple_of(base, 16), size)

    gots = (got0, got1, got2, got3, got4)
    sums_of = (sum0, sum1, sum2, sum3)

    def double(spot_ref, rows, chunk, slots, send, recv):
        for e, peer in enumerate(w_peers):
            move = remote(spot_ref.at[chunk, rows], slots(e), send(e), recv(e), peer)
            move.start()
            move.wait()
            spot_ref[chunk, rows, :] = add(spot_ref[chunk, rows, :], slots(e)[...])

    def halve(n, order):
        chunk, first_row = n // 3, (n % 3) * 512
        stages = [halvings[name] for name in ("core",) + order]
        held, offset, base = part.at[chunk], first_row, first_row
        bases = []
        for level, (digit, peer) in enumerate(stages):
            size = 256 >> level
            move = remote(
                held.at[piece(offset + (1 - digit) * size, size)], gots[level].at[n],
                rs_send.at[level, n], rs_recv.at[level, n], peer,
            )
            move.start()
            yield
            move.wait()
            mine = held[piece(offset + digit * size, size), :]
            base = base + digit * size
            bases.append((base, size))
            if level < 4:
                sums_of[level][n] = add(mine, gots[level][n])
                held, offset = sums_of[level].at[n], 0
            else:
                full[chunk, piece(base, size), :] = add(mine, gots[level][n])
        double(
            full, piece(base, 16), chunk,
            lambda e: got4.at[6 + e * 6 + n],
            lambda e: rs_send.at[5 + e, n], lambda e: rs_recv.at[5 + e, n],
        )
        for level in (4, 3, 2, 1, 0):
            base, size = bases[level]
            spot = full.at[chunk, piece(base, size)]
            move = remote(spot, spot, ag_send.at[level, n], ag_recv.at[level, n], stages[level][1])
            move.start()
            yield
            move.wait()

    plane = 2 * yy + xx
    plane_peers = [(x_peer, yy * 2 + 1 - xx), (y_peer, (1 - yy) * 2 + xx), (xy_peer, (1 - yy) * 2 + 1 - xx)]

    def spread(b):
        rows = b * D
        move = remote(
            part.at[2, piece(rows + (1 - core) * 192, 192)], blk0.at[b],
            blk_send.at[0, b], blk_recv.at[0, b], core_peer,
        )
        move.start()
        yield
        move.wait()
        blk_sum[b] = add(part[2, piece(rows + core * 192, 192), :], blk0[b])
        moves = []
        for j, (peer, where) in enumerate(plane_peers):
            move = remote(
                blk_sum.at[b, piece(where * 48, 48)], blk1.at[b, j],
                blk_send.at[1 + j, b], blk_recv.at[1 + j, b], peer,
            )
            move.start()
            moves.append(move)
        yield
        total = blk_sum[b, piece(plane * 48, 48), :].astype(F32)
        for j in range(3):
            moves[j].wait()
            total = total + blk1[b, j].astype(F32)
        blk2[b, zz] = total.astype(BF16)
        moves = []
        for j, peer in enumerate(z_peers):
            move = remote(
                blk2.at[b, zz], blk2.at[b, zz], blk_send.at[4 + j, b], blk_recv.at[4 + j, b], peer,
            )
            move.start()
            moves.append(move)
        yield
        for move in moves:
            move.wait()
        mine = piece(rows + core * 192 + plane * 48, 48)
        full[2, mine, :] = (
            (blk2[b, 0].astype(F32) + blk2[b, 1].astype(F32))
            + (blk2[b, 2].astype(F32) + blk2[b, 3].astype(F32))
        ).astype(BF16)
        double(
            full, mine, 2,
            lambda e: blk2.at[b, 4 + e],
            lambda e: blk_send.at[11 + e, b], lambda e: blk_recv.at[11 + e, b],
        )
        moves = []
        for j, (peer, _) in enumerate(plane_peers):
            spot = full.at[2, mine]
            move = remote(spot, spot, blk_send.at[7 + j, b], blk_recv.at[7 + j, b], peer)
            move.start()
            moves.append(move)
        yield
        for move in moves:
            move.wait()
        spot = full.at[2, piece(rows + core * 192, 192)]
        move = remote(spot, spot, blk_send.at[10, b], blk_recv.at[10, b], core_peer)
        move.start()
        yield
        move.wait()

    def vectors():
        for step, peer in enumerate((core_peer, y_peer, x_peer)):
            move = remote(small, small_got.at[step], sm_send.at[step], sm_recv.at[step], peer)
            move.start()
            yield
            move.wait()
            small[...] = small[...] + small_got[step]
        small_z[zz] = small[...]
        moves = []
        for j, peer in enumerate(z_peers):
            move = remote(small_z.at[zz], small_z.at[zz], sm_send.at[3 + j], sm_recv.at[3 + j], peer)
            move.start()
            moves.append(move)
        yield
        for move in moves:
            move.wait()
        small[...] = (small_z[0] + small_z[1]) + (small_z[2] + small_z[3])
        for e, peer in enumerate(w_peers):
            move = remote(small, small_got.at[3 + e], sm_send.at[6 + e], sm_recv.at[6 + e], peer)
            move.start()
            move.wait()
            small[...] = small[...] + small_got[3 + e]

    agenda = []

    def launch(way, start, offsets):
        for i, offset in enumerate(offsets):
            agenda.append((start + offset, len(agenda), way))
        pump(start)

    def pump(now):
        agenda.sort(key=lambda entry: entry[:2])
        while agenda and agenda[0][0] <= now:
            _, _, way = agenda.pop(0)
            next(way, None)

    for i in range(3):
        part[0, i * 512 : (i + 1) * 512, :] = dot(
            active[:, i * 512 : (i + 1) * 512], g_low[...], TN
        ).astype(BF16)
        launch(halve(i, ORDERS[i]), 22.4 + 0.3 * i, HALVE_TIMES)

    def back_up(i, carry):
        cols = rows_of(i, 256)
        low = (dot(g_low[...], down_w[cols, :], NT) * slope[:, cols]).astype(BF16)
        g_up[:, cols] = low
        return carry

    lax.fori_loop(0, FF // 256, back_up, 0)
    pump(24.9)
    for i in range(4):
        small[i : i + 1, :] = jnp.sum(
            g_up[:, i * D : (i + 1) * D].astype(F32), axis=0, keepdims=True
        )
        part[1, i * D : (i + 1) * D, :] = dot(
            first_low[...], g_up[:, i * D : (i + 1) * D], TN
        ).astype(BF16)
    for i in range(3):
        launch(halve(3 + i, ORDERS[3 + i]), 25.6 + 0.1 * i, HALVE_TIMES)
    lower[...] = dot(g_up[...], up_w[...], NT)

    def norm_one_back(i, carry):
        gain_sum, bias_sum, out_sum = carry
        rows = rows_of(i, 128)
        grad = gsum[rows, :] + lower[rows, :]
        normal = y1[rows, :]
        grad_in = norm_back(grad, normal, r1[rows, :], gain_one)
        g_hid[rows, :] = grad_in
        low = grad_in.astype(BF16)
        g_low[rows, :] = low
        return (
            gain_sum + jnp.sum(grad * normal, axis=0, keepdims=True),
            bias_sum + jnp.sum(grad, axis=0, keepdims=True),
            out_sum + jnp.sum(low.astype(F32), axis=0, keepdims=True),
        )

    gain1, bias1, out_sum = lax.fori_loop(0, 4, norm_one_back, (zero_row, zero_row, zero_row))
    pump(26.6)
    small[5:6, :] = out_sum
    small[8:9, :] = gain1
    small[9:10, :] = bias1
    small[12:16, :] = jnp.zeros((4, D), F32)

    part[2, :D, :] = dot(c_t[...], g_low[...], NN).astype(BF16)
    launch(spread(0), 27.3, SPREAD_TIMES)
    gc_t[...] = dot(out_w[...], g_low[...], NT).astype(BF16)

    def attend_back(g, i):
        h = 4 * g + i
        rows = slice(h * HD, (h + 1) * HD)
        inverse = inv[h][:1, :]
        grad_c = (gc_t[rows, :].astype(F32) * inverse).astype(BF16)
        inner = jnp.sum(grad_c.astype(F32) * c_t[rows, :].astype(F32), axis=0, keepdims=True)
        grad_w = dot(v_x[h * VROWS : h * VROWS + HD, :], grad_c, TN)
        weights = probs[h]
        grad_s = (weights.astype(F32) * (grad_w - inner)).astype(BF16)
        base = g * D + i * HD
        gj_t[base : base + HD, :] = (dot(kz_t[rows, :], grad_s, NN) * SCALE).astype(BF16)
        gk = jnp.where(lane_valid, dot(q_t[rows, :], grad_s, NT) * SCALE, 0.0)
        gj_t[base + 128 : base + 128 + HD, :] = gk.astype(BF16)
        gv = jnp.where(lane_valid, dot(grad_c, weights, NT), 0.0)
        gj_t[base + 256 : base + 256 + HD, :] = gv.astype(BF16)

    clock = 27.6
    for g in range(GROUPS):
        for i in range(4):
            attend_back(g, i)
            clock += 0.67
            if i % 2 == 1:
                pump(clock)
        both = dot(x_t[...], gj_t[g * D : (g + 1) * D, :], NT)
        part[2, (g + 1) * D : (g + 2) * D, :] = both[:D, :].astype(BF16)
        small[6:7, g * 128 : (g + 1) * 128] = both[D : D + 1, :128]
        small[7:8, g * 128 : (g + 1) * 128] = both[D : D + 1, 256:]
        clock += 0.3
        launch(spread(g + 1), clock, SPREAD_TIMES)
    launch(vectors(), clock, VECTOR_TIMES)

    igr[...] = (g_hid[...] + dot(gj_t[...], qkv_t[...], TN)).astype(BF16)
    for i, peer in enumerate(seq_peers):
        move = remote(
            igr.at[pl.ds(pl.multiple_of(peer * 128, 128), 128)], igrad_ref.at[sq, 0],
            out_send.at[1, i], out_recv.at[1, i], (dp, peer),
        )
        move.start()
        out_moves.append(move)
    own_i = pltpu.make_async_copy(igr.at[own_rows], igrad_ref.at[sq, 0], loc_sem.at[3])
    own_i.start()

    pump(1e9)
    small_ref[...] = small[...]
    for move in out_moves:
        move.wait()
    pooled_ref[...] = pool[...]
    own_b.wait()
    own_i.wait()


def finish_kernel(
    grads_ref, small_ref, pool_ref, bl_ref, ig_ref,
    block_ref, pooled_ref, igrad_ref, qkv_ref, qb_ref, vb_ref, out_ref, ob_ref, g1_ref, b1_ref,
    up_ref, ub_ref, down_ref, db_ref, g2_ref, b2_ref,
    wide, out_sem, sem,
):
    moves = []
    for i, (src, dst) in enumerate(((bl_ref, block_ref), (ig_ref, igrad_ref))):
        move = pltpu.make_async_copy(src, dst, sem.at[i])
        move.start()
        moves.append(move)
    for i in range(4):
        ub_ref[i * D : (i + 1) * D] = small_ref[i, :]
    for m in range(4):
        pooled_ref[m] = pool_ref[m, :1, :]
    for row, ref in ((4, db_ref), (5, ob_ref), (6, qb_ref), (7, vb_ref), (8, g1_ref), (9, b1_ref), (10, g2_ref), (11, b2_ref)):
        ref[...] = small_ref[row, :]
    for i in range(12):
        wide[i] = grads_ref[i // 4, (i % 4) * D : (i % 4 + 1) * D, :].astype(F32)
        span = pl.ds((i % 4) * D, D)
        if i < 4:
            copies = [(wide.at[i], down_ref.at[span])]
        elif i < 8:
            copies = [(wide.at[i], up_ref.at[:, span])]
        elif i == 8:
            copies = [(wide.at[i], out_ref)]
        else:
            copies = [
                (wide.at[i, :, pl.ds(j * 128, 128)], qkv_ref.at[:, pl.ds(j * D + (i - 9) * 128, 128)])
                for j in range(3)
            ]
        for j, (src, dst) in enumerate(copies):
            move = pltpu.make_async_copy(src, dst, out_sem.at[i, j])
            move.start()
            moves.append(move)
    for move in moves:
        move.wait()


def body(
    ndp,
    inputs, lengths, cotangent, pool_cotangent, qkv_weight, query_bias, value_bias,
    out_weight, out_bias, norm1_gain, norm1_bias, up_weight, up_bias, down_weight,
    down_bias, norm2_gain, norm2_bias,
):
    any_spec = pl.BlockSpec(memory_space=pltpu.HBM)
    vmem = pl.BlockSpec(memory_space=pltpu.VMEM)
    smem = pl.BlockSpec(memory_space=pltpu.SMEM)
    extra = max(ndp.bit_length() - 4, 0)

    def v(*shape, dtype=BF16):
        return pltpu.VMEM(shape, dtype)

    dma = pltpu.SemaphoreType.DMA
    args = (
        inputs, lengths.T, cotangent, jnp.transpose(pool_cotangent, (1, 0, 2)),
        qkv_weight, query_bias, value_bias, out_weight, out_bias,
        norm1_gain, norm1_bias, up_weight, up_bias, down_weight, down_bias,
        norm2_gain, norm2_bias,
    )
    in_specs = [
        any_spec, smem, any_spec, vmem,
        any_spec, vmem, vmem, any_spec, vmem,
        vmem, vmem, any_spec, vmem, any_spec, vmem,
        vmem, vmem,
    ]
    results = pl.pallas_call(
        functools.partial(kernel, ndp),
        out_shape=(
            v(*inputs.shape), v(4, 8, D, dtype=F32), v(*inputs.shape), v(CHUNKS, ROWS, D), v(16, D, dtype=F32),
        ),
        in_specs=in_specs,
        out_specs=(vmem,) * 5,
        scratch_shapes=[
            v(512, D), v(512, D), v(D, 3 * D), v(D, D), v(D, FF), v(FF, D), v(3 * D, D), v(D + 16, 512),
            v(D, 512), v(D, 512), v(D, 512), v(H * VROWS, 512), v(H, 512, 512), v(H, 8, 512, dtype=F32),
            v(D, 512), v(512, D, dtype=F32), v(512, 1, dtype=F32), v(512, D), v(512, FF), v(512, FF, dtype=F32),
            v(512, D, dtype=F32), v(512, D, dtype=F32), v(512, D), v(512, FF), v(512, D, dtype=F32),
            v(D, 512), v(3 * D, 512), v(512, D), v(512, D), v(4, 8, D, dtype=F32),
            v(CHUNKS, ROWS, D), v(6, 256, D), v(6, 128, D), v(6, 64, D), v(6, 32, D), v(6 + 6 * extra, 16, D),
            v(6, 256, D), v(6, 128, D), v(6, 64, D), v(6, 32, D),
            v(4, 192, D), v(4, 3, 48, D), v(4, 4 + extra, 48, D), v(4, 192, D),
            v(16, D, dtype=F32), v(3 + extra, 16, D, dtype=F32), v(4, 16, D, dtype=F32), v(1, FF, dtype=F32),
            dma((4,)), dma((4,)), dma((2, 3)), dma((2, 3)), dma((2, 3)), dma((2, 3)), dma((3,)), dma((3,)),
            dma((5 + extra, 6)), dma((5 + extra, 6)), dma((5, 6)), dma((5, 6)),
            dma((11 + extra, 4)), dma((11 + extra, 4)), dma((6 + extra,)), dma((6 + extra,)),
        ],
        compiler_params=pltpu.CompilerParams(
            collective_id=0, has_side_effects=True, vmem_limit_bytes=56 * 2**20
        ),
    )(*args)
    block, pooled, igrad, grads, small = results

    def shape(*dims, dtype=F32):
        return jax.ShapeDtypeStruct(dims, dtype)

    outs = pl.pallas_call(
        finish_kernel,
        out_shape=(
            shape(*inputs.shape, dtype=BF16), shape(4, 1, D), shape(*inputs.shape, dtype=BF16),
            shape(D, 3 * D), shape(D), shape(D), shape(D, D), shape(D), shape(D), shape(D),
            shape(D, FF), shape(FF), shape(FF, D), shape(D), shape(D), shape(D),
        ),
        in_specs=[vmem] * 5,
        out_specs=(
            any_spec, vmem, any_spec, any_spec, vmem, vmem, any_spec, vmem, vmem, vmem,
            any_spec, vmem, any_spec, vmem, vmem, vmem,
        ),
        scratch_shapes=[v(12, D, D, dtype=F32), dma((12, 3)), dma((2,))],
        compiler_params=pltpu.CompilerParams(vmem_limit_bytes=24 * 2**20),
    )(grads, small, pooled, block, igrad)
    return outs


def solution(mesh):
    whole = P()
    return jax.shard_map(
        functools.partial(body, mesh.shape["dp"]),
        mesh=mesh,
        in_specs=(
            P(None, "dp", "seq", None), P(None, "dp"), P(None, "dp", "seq", None), P(None, "dp", None),
        ) + (whole,) * 13,
        out_specs=(
            P(None, "dp", "seq", None), P(None, "dp", None), P(None, "dp", "seq", None),
        ) + (whole,) * 13,
        check_vma=False,
    )
```

```python
import functools

import jax
import jax.numpy as jnp
from jax import lax
from jax.experimental import pallas as pl
from jax.experimental.pallas import tpu as pltpu
from jax.sharding import PartitionSpec as P

H = 12
HD = 32
D = 384
FF = 1536
EPS = 1e-6
F32 = jnp.float32
BF16 = jnp.bfloat16
MESH = pl.DeviceIdType.MESH
NN = (((1,), (0,)), ((), ()))
NT = (((1,), (1,)), ((), ()))
TN = (((0,), (0,)), ((), ()))
LOG2E = 1.4426950408889634
SCALE = HD**-0.5
VROWS = HD + 16
CHUNKS = 3
ROWS = 1536
GROUPS = 3
PLAN = (
    (0, 512, ("core", "z1", "xy", "z2")),
    (512, 512, ("core", "z1", "z2", "xy")),
    (1024, 512, ("core", "xy", "z")),
    (1536, 512, ("core", "z1", "xy", "z2")),
    (2048, 512, ("core", "x", "y", "z")),
    (2560, 512, ("core", "z", "x", "y")),
    (3072, 512, ("core", "xy", "z")),
    (3584, 384, ("core", "xy", "all_z")),
    (3968, 384, ("core", "xy", "all_z")),
    (4352, 256, ("core", "xy", "all_z")),
)
SCHEDULE = (
    -1, -1, -1, 0, 1, -1, 2, -1, -1, -1, -1, 3, 4, 5, 0, -1, 10, -1, 1, 2, -1, -1, -1, 4, 3, 6, -1, 0,
    -1, 10, -1, -1, 5, 4, 1, 7, -1, 3, -1, 0, 2, -1, 6, 5, 8, -1, 1, 10, 4, -1, 3, -1, 7, 5, 9, 0, 11,
    2, 8, 6, 1, 5, 4, 3, 9, 12, 0, 11, 7, 5, 2, 4, 2, 8, 3, 6, 1, 0, 4, 0, 9, 4, 7, 11, 7, 8, 3, 8, 6,
    3, 5, 9, 1, 6, 5, 9, 1,
)


def dot(left, right, dims):
    return lax.dot_general(left, right, dims, preferred_element_type=F32)


def gelu_and_slope(upper):
    cdf = 0.5 * (1.0 + lax.erf(upper * 2.0**-0.5))
    density = jnp.exp2((-0.5 * LOG2E) * (upper * upper)) * (2.0 * jnp.pi) ** -0.5
    return upper * cdf, cdf + upper * density


def layer_norm(values):
    centre = values - jnp.mean(values, axis=-1, keepdims=True)
    inverse = lax.rsqrt(jnp.mean(centre * centre, axis=-1, keepdims=True) + EPS)
    return centre * inverse, inverse


def norm_back(grad_out, normal, inverse, gain):
    scaled = grad_out * gain
    return inverse * (
        scaled
        - jnp.mean(scaled, axis=-1, keepdims=True)
        - normal * jnp.mean(scaled * normal, axis=-1, keepdims=True)
    )


def kernel(
    ndp,
    inputs_ref, lengths_ref, cot_ref, pool_ref,
    qkv_hbm, qb_ref, vb_ref, out_hbm, ob_ref, g1_ref, b1_ref,
    up_hbm, ub_ref, down_hbm, db_ref, g2_ref, b2_ref,
    block_ref, pooled_ref, igrad_ref, full, small_ref,
    x, cot, qkv_w, out_w, up_w, down_w, qkv_t,
    q_t, kd_t, kz_t, v_x, probs, inv, c_t, y1, r1, first_low, active, slope,
    lower, gsum, g_low, g_up, g_hid, gc_t, gj_t, bout, igr, pool,
    part, small, late, up_row,
    w_sem, loc_sem, in_send, in_recv, out_send, out_recv, pool_send, pool_recv,
    s_a, s_b, gs_t, gs_n, p_n, *travel_refs,
):
    dp = lax.axis_index("dp")
    sq = lax.axis_index("seq")
    core = lax.rem(sq, 2)
    yy = lax.div(sq, 2)
    xx = lax.rem(dp, 2)
    zz = lax.rem(lax.div(dp, 2), 4)
    extra = []
    bit = 8
    while bit < ndp:
        extra.append(bit)
        bit *= 2

    def flip(index, amount):
        digit = lax.rem(lax.div(index, amount), 2)
        return index + amount * (1 - 2 * digit)

    seq_peers = [lax.rem(sq + step, 4) for step in (1, 2, 3)]
    core_peer = (dp, flip(sq, 1))
    y_peer = (dp, flip(sq, 2))
    x_peer = (flip(dp, 1), sq)
    xy_peer = (flip(dp, 1), flip(sq, 2))
    z_peers = [(dp + 2 * (lax.rem(zz + step, 4) - zz), sq) for step in (1, 2, 3)]
    w_peers = [(flip(dp, amount), sq) for amount in extra]
    greeted = [(dp, peer) for peer in seq_peers] + [x_peer, xy_peer] + z_peers + w_peers
    halvings = {
        "core": (core, core_peer),
        "y": (yy, y_peer),
        "x": (xx, x_peer),
        "z1": (lax.rem(zz, 2), (flip(dp, 2), sq)),
        "z2": (lax.div(zz, 2), (flip(dp, 4), sq)),
    }

    loads = [
        pltpu.make_async_copy(src, dst, w_sem.at[i])
        for i, (src, dst) in enumerate(
            [(qkv_hbm, qkv_w), (out_hbm, out_w), (up_hbm, up_w), (down_hbm, down_w)]
        )
    ]
    for load in loads:
        load.start()
    own_rows = pl.ds(pl.multiple_of(sq * 128, 128), 128)
    own_x = pltpu.make_async_copy(inputs_ref.at[sq, 0], x.at[own_rows], loc_sem.at[0])
    own_c = pltpu.make_async_copy(cot_ref.at[sq, 0], cot.at[own_rows], loc_sem.at[1])
    own_x.start()
    own_c.start()

    barrier = pltpu.get_barrier_semaphore()
    for peer in greeted:
        pl.semaphore_signal(barrier, inc=1, device_id=peer, device_id_type=MESH)
    pl.semaphore_wait(barrier, len(greeted))

    def remote(src, dst, send, recv, peer):
        return pltpu.make_async_remote_copy(
            src_ref=src, dst_ref=dst, send_sem=send, recv_sem=recv,
            device_id=peer, device_id_type=MESH,
        )

    x_moves, c_moves = [], []
    for which, (src, dst, moves) in enumerate(((inputs_ref, x, x_moves), (cot_ref, cot, c_moves))):
        for i, peer in enumerate(seq_peers):
            move = remote(
                src.at[peer, 0], dst.at[own_rows],
                in_send.at[which, i], in_recv.at[which, i], (dp, peer),
            )
            moves.append(move)
    for move in x_moves:
        move.start()

    span = lengths_ref[0, sq]
    query_bias, value_bias, out_bias, gain_one, bias_one, up_bias, down_bias, gain_two, bias_two = (
        ref[...].reshape(1, -1)
        for ref in (qb_ref, vb_ref, ob_ref, g1_ref, b1_ref, ub_ref, db_ref, g2_ref, b2_ref)
    )
    up_row[...] = up_bias
    count = span.astype(F32)
    lane_valid = lax.broadcasted_iota(jnp.int32, (1, 512), 1) < span

    loads[0].wait()

    for i in range(3):
        for g in range(GROUPS):
            turned = qkv_w[:, i * D + g * 128 : i * D + (g + 1) * 128].T
            for j in range(2):
                first = (2 * g + j) * 192 + i * 64
                qkv_t[first : first + 64, :] = turned[j * 64 : (j + 1) * 64]
    own_x.wait()
    for move in x_moves:
        move.wait()
    for move in c_moves:
        move.start()

    qcol = jnp.broadcast_to(query_bias, (8, D)).T[:, :1]
    vcol = jnp.broadcast_to(value_bias, (8, D)).T[:, :1]
    ones_row = jnp.broadcast_to(jnp.where(lane_valid, 1.0, 0.0), (16, 512)).astype(BF16)
    for g in range(GROUPS):
        joined = dot(qkv_t[g * D : (g + 1) * D, :], x[...], NT)
        for j in range(2):
            feats = slice((2 * g + j) * 64, (2 * g + j + 1) * 64)
            first = j * 192
            q_t[feats, :] = (joined[first : first + 64] + qcol[feats]).astype(BF16)
            keys = joined[first + 64 : first + 128]
            kd_t[feats, :] = jnp.where(lane_valid, keys, keys[:, :1]).astype(BF16)
            kz_t[feats, :] = jnp.where(lane_valid, keys, 0.0).astype(BF16)
            values = jnp.where(lane_valid, joined[first + 128 : first + 192] + vcol[feats], 0.0).astype(BF16)
            for i in range(2):
                h = 4 * g + 2 * j + i
                v_x[h * VROWS : h * VROWS + HD, :] = values[i * HD : (i + 1) * HD, :]
                v_x[h * VROWS + HD : (h + 1) * VROWS, :] = ones_row

    def score(h):
        rows = slice(h * HD, (h + 1) * HD)
        return dot(kd_t[rows, :], q_t[rows, :], TN)

    def soften(scores):
        peak = jnp.max(scores, axis=0, keepdims=True)
        return jnp.exp2(scores * (SCALE * LOG2E) - peak * (SCALE * LOG2E)).astype(BF16)

    def gather(h, raised):
        both = dot(v_x[h * VROWS : (h + 1) * VROWS, :], raised, NN)
        inverse = 1.0 / both[HD : HD + 1, :]
        inv[h] = jnp.broadcast_to(inverse, (8, 512))
        c_t[h * HD : (h + 1) * HD, :] = (both[:HD, :] * inverse).astype(BF16)

    sbufs = (s_a, s_b)
    s_a[...] = score(0)
    for h in range(H):
        if h + 1 < H:
            sbufs[(h + 1) % 2][...] = score(h + 1)
        for q in range(4):
            probs[h, :, q * 128 : (q + 1) * 128] = soften(sbufs[h % 2][:, q * 128 : (q + 1) * 128])
        gather(h, probs[h])

    loads[1].wait()

    lower[...] = dot(c_t[...], out_w[...], TN)

    def norm_one(i):
        rows = slice(i * 128, (i + 1) * 128)
        normal, inverse = layer_norm(x[rows, :].astype(F32) + lower[rows, :] + out_bias)
        y1[rows, :] = normal
        r1[rows, :] = inverse
        first_low[rows, :] = (normal * gain_one + bias_one).astype(BF16)

    for i in range(4):
        norm_one(i)
    loads[2].wait()

    def raise_up(i):
        cols = slice(i * 256, (i + 1) * 256)
        upper = dot(first_low[...], up_w[:, cols], NN) + up_row[:, cols]
        act, slp = gelu_and_slope(upper)
        active[:, cols] = act.astype(BF16)
        slope[:, cols] = slp

    for i in range(FF // 256):
        raise_up(i)
    loads[3].wait()
    lower[...] = dot(active[...], down_w[...], NN)
    own_c.wait()
    for move in c_moves:
        move.wait()
    chosen = lax.broadcasted_iota(jnp.int32, (4, D), 0) == sq
    pool_share = jnp.sum(jnp.where(chosen, pool_ref[0].astype(F32), 0.0), axis=0, keepdims=True) / count

    zero_row = jnp.zeros((1, D), F32)

    def norm_two(i, carry):
        sums, gain_sum, bias_sum, down_sum = carry
        rows = slice(i * 128, (i + 1) * 128)
        firsts = y1[rows, :] * gain_one + bias_one
        normal, inverse = layer_norm(firsts + lower[rows, :] + down_bias)
        here = lax.broadcasted_iota(jnp.int32, (128, 1), 0) + i * 128 < span
        masked = jnp.where(here, normal * gain_two + bias_two, 0.0)
        bout[rows, :] = masked.astype(BF16)
        grad = jnp.where(here, cot[rows, :].astype(F32) + pool_share, 0.0)
        grad_in = norm_back(grad, normal, inverse, gain_two)
        gsum[rows, :] = grad_in
        low = grad_in.astype(BF16)
        g_low[rows, :] = low
        return (
            sums + jnp.sum(masked, axis=0, keepdims=True),
            gain_sum + jnp.sum(grad * normal, axis=0, keepdims=True),
            bias_sum + jnp.sum(grad, axis=0, keepdims=True),
            down_sum + jnp.sum(low.astype(F32), axis=0, keepdims=True),
        )

    carry = (zero_row, zero_row, zero_row, zero_row)
    for i in range(4):
        carry = norm_two(i, carry)
    sums, gain2, bias2, down_sum = carry
    pool[sq] = jnp.broadcast_to(sums / count, (8, D))
    small[4:5, :] = down_sum
    small[10:11, :] = gain2
    small[11:12, :] = bias2

    out_moves = []
    for i, peer in enumerate(seq_peers):
        move = remote(
            bout.at[pl.ds(pl.multiple_of(peer * 128, 128), 128)], block_ref.at[sq, 0],
            out_send.at[0, i], out_recv.at[0, i], (dp, peer),
        )
        move.start()
        out_moves.append(move)
        move = remote(pool.at[sq], pool.at[sq], pool_send.at[i], pool_recv.at[i], (dp, peer))
        move.start()
        out_moves.append(move)
    own_b = pltpu.make_async_copy(bout.at[own_rows], block_ref.at[sq, 0], loc_sem.at[2])
    own_b.start()

    def add(left, right):
        return (left.astype(F32) + right.astype(F32)).astype(BF16)

    def piece(base, size):
        return pl.ds(base if isinstance(base, int) else pl.multiple_of(base, 16), size)

    plane = 2 * yy + xx
    plane_peers = [(x_peer, yy * 2 + 1 - xx), (y_peer, (1 - yy) * 2 + xx), (xy_peer, (1 - yy) * 2 + 1 - xx)]
    z_places = [(peer, lax.rem(zz + 1 + j, 4)) for j, peer in enumerate(z_peers)]
    groups = {name: (digit, [(peer, 1 - digit)]) for name, (digit, peer) in halvings.items()}
    groups["xy"] = (plane, plane_peers)
    groups["z"] = groups["all_z"] = (zz, z_places)
    refs = list(travel_refs)

    def travel(first, rows, way):
        levels = len(way)
        gots = [refs.pop(0) for _ in range(levels)]
        sums = [refs.pop(0) for _ in range(levels - 1)]
        more = refs.pop(0) if w_peers else None
        send, recv = refs.pop(0), refs.pop(0)
        return steps_of(first, rows, way, gots, sums, more, send, recv)

    def steps_of(first, rows, way, gots, sums, more, send, recv):
        used = iter(range(100))
        held, offset, base, size = part, first, first, rows
        places = []
        for level, name in enumerate(way):
            index, peers = groups[name]
            moves = []
            if name == "all_z":
                gots[level][index] = held[piece(offset, size), :]
                mine = gots[level].at[index]
                for peer, _ in peers:
                    n = next(used)
                    moves.append(remote(mine, mine, send.at[n], recv.at[n], peer))
            else:
                size //= len(peers) + 1
                for j, (peer, where) in enumerate(peers):
                    n = next(used)
                    moves.append(remote(
                        held.at[piece(offset + where * size, size)], gots[level].at[j],
                        send.at[n], recv.at[n], peer,
                    ))
            for move in moves:
                move.start()
            yield
            for move in moves:
                move.wait()
            if name == "all_z":
                terms = [gots[level][j].astype(F32) for j in range(4)]
                total = (terms[0] + terms[1]) + (terms[2] + terms[3])
            else:
                total = held[piece(offset + index * size, size), :].astype(F32)
                for j in range(len(peers)):
                    total = total + gots[level][j].astype(F32)
                base = base + index * size
                places.append((base, size, peers))
            if level < len(way) - 1:
                sums[level][...] = total.astype(BF16)
                held, offset = sums[level], 0
            else:
                full[piece(base, size), :] = total.astype(BF16)
        for e, peer in enumerate(w_peers):
            n = next(used)
            spot = full.at[piece(base, size)]
            move = remote(spot, more.at[e], send.at[n], recv.at[n], peer)
            move.start()
            move.wait()
            full[piece(base, size), :] = add(full[piece(base, size), :], more[e])
        for base, size, peers in reversed(places):
            moves = []
            for peer, _ in peers:
                n = next(used)
                spot = full.at[piece(base, size)]
                moves.append(remote(spot, spot, send.at[n], recv.at[n], peer))
            for move in moves:
                move.start()
            yield
            for move in moves:
                move.wait()

    def vectors(mine, got, planes, zs, more, send, recv):
        move = remote(mine, got, send.at[0], recv.at[0], core_peer)
        move.start()
        yield
        move.wait()
        total = mine[...] + got[...]
        for slots, index, peers, n in ((planes, plane, plane_peers, 1), (zs, zz, z_places, 4)):
            slots[index] = total
            moves = [
                remote(slots.at[index], slots.at[index], send.at[n + j], recv.at[n + j], peer)
                for j, (peer, _) in enumerate(peers)
            ]
            for move in moves:
                move.start()
            yield
            for move in moves:
                move.wait()
            total = (slots[0] + slots[1]) + (slots[2] + slots[3])
        mine[...] = total
        for e, peer in enumerate(w_peers):
            move = remote(mine, more.at[e], send.at[7 + e], recv.at[7 + e], peer)
            move.start()
            move.wait()
            mine[...] = mine[...] + more[e]

    def back_home():
        for i, peer in enumerate(seq_peers):
            move = remote(
                igr.at[pl.ds(pl.multiple_of(peer * 128, 128), 128)], igrad_ref.at[sq, 0],
                out_send.at[1, i], out_recv.at[1, i], (dp, peer),
            )
            move.start()
            out_moves.append(move)
        yield

    def vector_refs():
        got, planes, zs = refs.pop(0), refs.pop(0), refs.pop(0)
        more = refs.pop(0) if w_peers else None
        return got, planes, zs, more, refs.pop(0), refs.pop(0)

    travels = [travel(*entry) for entry in PLAN]
    travels += [vectors(small, *vector_refs()), vectors(late, *vector_refs()), back_home()]
    agenda = list(SCHEDULE)

    def go():
        while agenda and agenda[0] >= 0:
            next(travels[agenda.pop(0)], None)
        if agenda:
            agenda.pop(0)

    def launch(n):
        next(travels[n])

    for i in range(3):
        part[i * 512 : (i + 1) * 512, :] = dot(
            active[:, i * 512 : (i + 1) * 512], g_low[...], TN
        ).astype(BF16)
        launch(i)
        go()

    for j in range(3):
        for i in (2 * j, 2 * j + 1):
            cols = slice(i * 256, (i + 1) * 256)
            g_up[:, cols] = (dot(g_low[...], down_w[cols, :], NT) * slope[:, cols]).astype(BF16)
        go()
    for i in range(4):
        small[i : i + 1, :] = jnp.sum(
            g_up[:, i * D : (i + 1) * D].astype(F32), axis=0, keepdims=True
        )
        part[ROWS + i * D : ROWS + (i + 1) * D, :] = dot(
            first_low[...], g_up[:, i * D : (i + 1) * D], TN
        ).astype(BF16)
    for i in range(3):
        launch(3 + i)
    go()
    lower[...] = dot(g_up[...], up_w[...], NT)
    go()

    def norm_one_back(i, carry):
        gain_sum, bias_sum, out_sum = carry
        rows = slice(i * 128, (i + 1) * 128)
        grad = gsum[rows, :] + lower[rows, :]
        normal = y1[rows, :]
        grad_in = norm_back(grad, normal, r1[rows, :], gain_one)
        g_hid[rows, :] = grad_in
        low = grad_in.astype(BF16)
        g_low[rows, :] = low
        return (
            gain_sum + jnp.sum(grad * normal, axis=0, keepdims=True),
            bias_sum + jnp.sum(grad, axis=0, keepdims=True),
            out_sum + jnp.sum(low.astype(F32), axis=0, keepdims=True),
        )

    carry = (zero_row, zero_row, zero_row)
    for i in range(4):
        carry = norm_one_back(i, carry)
    gain1, bias1, out_sum = carry
    small[5:6, :] = out_sum
    small[8:9, :] = gain1
    small[9:10, :] = bias1
    small[6:8, :] = jnp.zeros((2, D), F32)
    small[12:16, :] = jnp.zeros((4, D), F32)
    launch(len(PLAN))
    go()

    part[2 * ROWS : 2 * ROWS + D, :] = dot(c_t[...], g_low[...], NN).astype(BF16)
    gc_t[...] = dot(out_w[...], g_low[...], NT).astype(BF16)
    go()

    def scale_c(h):
        rows = slice(h * HD, (h + 1) * HD)
        return (gc_t[rows, :].astype(F32) * inv[h][:1, :]).astype(BF16)

    def grad_weights(h):
        sbufs[h % 2][...] = dot(v_x[h * VROWS : h * VROWS + HD, :], scale_c(h), TN)

    grad_weights(0)

    def attend_back(h):
        rows = slice(h * HD, (h + 1) * HD)
        if h + 1 < H:
            grad_weights(h + 1)
        grad_c = scale_c(h)
        inner = jnp.sum(grad_c.astype(F32) * c_t[rows, :].astype(F32), axis=0, keepdims=True)
        weights = probs[h]
        gs_t[...] = (weights.astype(F32) * (sbufs[h % 2][...] - inner)).astype(BF16)
        gs_n[...] = gs_t[...].T
        p_n[...] = weights.T
        base = (h // 2) * 192 + (h % 2) * HD
        gv = jnp.where(lane_valid, dot(grad_c, p_n[...], NN), 0.0)
        gj_t[base + 128 : base + 128 + HD, :] = gv.astype(BF16)
        gj_t[base : base + HD, :] = (dot(kz_t[rows, :], gs_t[...], NN) * SCALE).astype(BF16)
        gk = jnp.where(lane_valid, dot(q_t[rows, :], gs_n[...], NN) * SCALE, 0.0)
        gj_t[base + 64 : base + 64 + HD, :] = gk.astype(BF16)

    for h in range(H):
        attend_back(h)
        if h % 2 == 1:
            first = (h // 2) * 192
            begin = 2 * ROWS + D + first
            part[begin : begin + 192, :] = dot(gj_t[first : first + 192, :], x[...], NN).astype(BF16)
            ready = begin + 192
            for n in range(6, len(PLAN)):
                if ready - 192 < PLAN[n][0] + PLAN[n][1] <= ready:
                    launch(n)
        go()
    query_sums, value_sums = [], []
    for g in range(H // 2):
        both = dot(jnp.ones((16, 512), BF16), gj_t[g * 192 : (g + 1) * 192, :], NT)
        query_sums.append(both[:1, :64])
        value_sums.append(both[:1, 128:])
    late[...] = jnp.concatenate(
        [
            jnp.concatenate(query_sums, axis=1),
            jnp.concatenate(value_sums, axis=1),
            jnp.zeros((6, D), F32),
        ],
        axis=0,
    )
    launch(len(PLAN) + 1)
    go()

    igr[...] = (g_hid[...] + dot(gj_t[...], qkv_t[...], TN)).astype(BF16)
    own_i = pltpu.make_async_copy(igr.at[own_rows], igrad_ref.at[sq, 0], loc_sem.at[3])
    own_i.start()
    go()

    go()
    small_ref[...] = small[...]
    small_ref[6:8, :] = late[:2, :]
    for move in out_moves:
        move.wait()
    pooled_ref[...] = pool[...]
    own_b.wait()
    own_i.wait()


def finish_kernel(
    grads_ref, small_ref, pool_ref, bl_ref, ig_ref,
    block_ref, pooled_ref, igrad_ref, qkv_ref, qb_ref, vb_ref, out_ref, ob_ref, g1_ref, b1_ref,
    up_ref, ub_ref, down_ref, db_ref, g2_ref, b2_ref,
    wide, out_sem, sem,
):
    moves = []
    for i, (src, dst) in enumerate(((bl_ref, block_ref), (ig_ref, igrad_ref))):
        move = pltpu.make_async_copy(src, dst, sem.at[i])
        move.start()
        moves.append(move)
    for i in range(4):
        ub_ref[i * D : (i + 1) * D] = small_ref[i, :]
    for m in range(4):
        pooled_ref[m] = pool_ref[m, :1, :]
    for row, ref in ((4, db_ref), (5, ob_ref), (6, qb_ref), (7, vb_ref), (8, g1_ref), (9, b1_ref), (10, g2_ref), (11, b2_ref)):
        ref[...] = small_ref[row, :]
    for i in range(12):
        if i < 9:
            wide[i] = grads_ref[i * D : (i + 1) * D, :].astype(F32)
        else:
            first = 9 * D + (i - 9) * 64
            turned = [grads_ref[first + g * 192 : first + g * 192 + 64, :] for g in range(H // 2)]
            wide[i] = jnp.concatenate(turned, axis=0).T.astype(F32)
        span = pl.ds((i % 4) * D, D)
        if i < 4:
            copies = [(wide.at[i], down_ref.at[span])]
        elif i < 8:
            copies = [(wide.at[i], up_ref.at[:, span])]
        elif i == 8:
            copies = [(wide.at[i], out_ref)]
        else:
            copies = [(wide.at[i], qkv_ref.at[:, pl.ds((i - 9) * D, D)])]
        for j, (src, dst) in enumerate(copies):
            move = pltpu.make_async_copy(src, dst, out_sem.at[i, j])
            move.start()
            moves.append(move)
    for move in moves:
        move.wait()


def travel_scratch(rows, way, extra):
    gots, sums, count = [], [], extra
    for name in way:
        peers = {"xy": 3, "z": 3, "all_z": 3}.get(name, 1)
        if name == "all_z":
            gots.append(pltpu.VMEM((4, rows, D), BF16))
            count += 3
        else:
            rows //= peers + 1
            gots.append(pltpu.VMEM((peers, rows, D), BF16))
            count += 2 * peers
        sums.append(pltpu.VMEM((rows, D), BF16))
    more = [pltpu.VMEM((extra, rows, D), BF16)] if extra else []
    return gots + sums[:-1] + more + [pltpu.SemaphoreType.DMA((count,))] * 2


def vector_scratch(rows, extra):
    slots = [pltpu.VMEM((rows, D), F32), pltpu.VMEM((4, rows, D), F32), pltpu.VMEM((4, rows, D), F32)]
    more = [pltpu.VMEM((extra, rows, D), F32)] if extra else []
    return slots + more + [pltpu.SemaphoreType.DMA((7 + extra,))] * 2


def body(
    ndp,
    inputs, lengths, cotangent, pool_cotangent, qkv_weight, query_bias, value_bias,
    out_weight, out_bias, norm1_gain, norm1_bias, up_weight, up_bias, down_weight,
    down_bias, norm2_gain, norm2_bias,
):
    any_spec = pl.BlockSpec(memory_space=pltpu.HBM)
    vmem = pl.BlockSpec(memory_space=pltpu.VMEM)
    smem = pl.BlockSpec(memory_space=pltpu.SMEM)
    extra = max(ndp.bit_length() - 4, 0)

    def v(*shape, dtype=BF16):
        return pltpu.VMEM(shape, dtype)

    dma = pltpu.SemaphoreType.DMA
    args = (
        inputs, lengths.T, cotangent, jnp.transpose(pool_cotangent, (1, 0, 2)),
        qkv_weight, query_bias, value_bias, out_weight, out_bias,
        norm1_gain, norm1_bias, up_weight, up_bias, down_weight, down_bias,
        norm2_gain, norm2_bias,
    )
    in_specs = [
        any_spec, smem, any_spec, vmem,
        any_spec, vmem, vmem, any_spec, vmem,
        vmem, vmem, any_spec, vmem, any_spec, vmem,
        vmem, vmem,
    ]
    results = pl.pallas_call(
        functools.partial(kernel, ndp),
        out_shape=(
            v(*inputs.shape), v(4, 8, D, dtype=F32), v(*inputs.shape), v(CHUNKS * ROWS, D), v(16, D, dtype=F32),
        ),
        in_specs=in_specs,
        out_specs=(vmem,) * 5,
        scratch_shapes=[
            v(512, D), v(512, D), v(D, 3 * D), v(D, D), v(D, FF), v(FF, D), v(3 * D, D),
            v(D, 512), v(D, 512), v(D, 512), v(H * VROWS, 512), v(H, 512, 512), v(H, 8, 512, dtype=F32),
            v(D, 512), v(512, D, dtype=F32), v(512, 1, dtype=F32), v(512, D), v(512, FF), v(512, FF, dtype=F32),
            v(512, D, dtype=F32), v(512, D, dtype=F32), v(512, D), v(512, FF), v(512, D, dtype=F32),
            v(D, 512), v(3 * D, 512), v(512, D), v(512, D), v(4, 8, D, dtype=F32),
            v(CHUNKS * ROWS, D),
            v(16, D, dtype=F32), v(8, D, dtype=F32), v(1, FF, dtype=F32),
            dma((4,)), dma((4,)), dma((2, 3)), dma((2, 3)), dma((2, 3)), dma((2, 3)), dma((3,)), dma((3,)),
            v(512, 512, dtype=F32), v(512, 512, dtype=F32), v(512, 512), v(512, 512), v(512, 512),
            *[item for _, rows, way in PLAN for item in travel_scratch(rows, way, extra)],
            *[item for rows in (16, 8) for item in vector_scratch(rows, extra)],
        ],
        compiler_params=pltpu.CompilerParams(
            collective_id=0, has_side_effects=True, vmem_limit_bytes=56 * 2**20
        ),
    )(*args)
    block, pooled, igrad, grads, small = results

    def shape(*dims, dtype=F32):
        return jax.ShapeDtypeStruct(dims, dtype)

    outs = pl.pallas_call(
        finish_kernel,
        out_shape=(
            shape(*inputs.shape, dtype=BF16), shape(4, 1, D), shape(*inputs.shape, dtype=BF16),
            shape(D, 3 * D), shape(D), shape(D), shape(D, D), shape(D), shape(D), shape(D),
            shape(D, FF), shape(FF), shape(FF, D), shape(D), shape(D), shape(D),
        ),
        in_specs=[vmem] * 5,
        out_specs=(
            any_spec, vmem, any_spec, any_spec, vmem, vmem, any_spec, vmem, vmem, vmem,
            any_spec, vmem, any_spec, vmem, vmem, vmem,
        ),
        scratch_shapes=[v(12, D, D, dtype=F32), dma((12, 3)), dma((2,))],
        compiler_params=pltpu.CompilerParams(vmem_limit_bytes=24 * 2**20),
    )(grads, small, pooled, block, igrad)
    return outs


def solution(mesh):
    whole = P()
    return jax.shard_map(
        functools.partial(body, mesh.shape["dp"]),
        mesh=mesh,
        in_specs=(
            P(None, "dp", "seq", None), P(None, "dp"), P(None, "dp", "seq", None), P(None, "dp", None),
        ) + (whole,) * 13,
        out_specs=(
            P(None, "dp", "seq", None), P(None, "dp", None), P(None, "dp", "seq", None),
        ) + (whole,) * 13,
        check_vma=False,
    )
```

```python
import functools

import jax
import jax.numpy as jnp
from jax import lax
from jax.experimental import pallas as pl
from jax.experimental.pallas import tpu as pltpu
from jax.sharding import PartitionSpec as P

H = 12
HD = 32
D = 384
FF = 1536
EPS = 1e-6
F32 = jnp.float32
BF16 = jnp.bfloat16
MESH = pl.DeviceIdType.MESH
NN = (((1,), (0,)), ((), ()))
NT = (((1,), (1,)), ((), ()))
TN = (((0,), (0,)), ((), ()))
LOG2E = 1.4426950408889634
SCALE = HD**-0.5
VROWS = HD + 16
CHUNKS = 3
ROWS = 1536
GROUPS = 3
WIDE = 2 * ROWS + D
PLAN = (
    (0, 512, ("core", "z1", "p", "q", "z2")),
    (512, 512, ("core", "p", "q", "z")),
    (1024, 512, ("core", "z1", "xy", "z2")),
    (1536, 512, ("core", "p", "q", "line")),
    (2048, 512, ("core", "p", "q", "z1", "z2")),
    (2560, 512, ("core", "z1", "z2", "xy")),
    (3072, 512, ("core", "p", "q", "line")),
    (3584, 256, ("core", "p", "q", "line")),
    (3840, 256, ("core", "p", "q", "line")),
    (4096, 256, ("core", "xy", "line")),
    (4352, 256, ("core", "xy", "all_z")),
)
SCHEDULE = (
    -1, -1, -1, 0, -1, 2, 1, -1, -1, -1, -1, 3, 4, 5, 0, -1, 1, 11, -1, 2, -1, -1, 3, -1, 5, 4, 6, 0,
    1, -1, 7, -1, 11, -1, -1, 4, 3, 2, -1, 6, 8, 0, 7, -1, 5, -1, -1, 4, 9, 6, 3, 1, -1, 8, 7, 10, -1,
    13, 5, 0, 2, 12, 11, 4, 6, 3, 8, 9, 7, 10, 1, 0, 2, 4, 3, 6, 8, 7, 9, 5, 12, 1, 0, 4, 8, 6, 9, 10,
    7, 2, 3, 1, 0, 8, 4, 5, 9, 6, 1, 7, 12, 10, 2, 3, 8, 10, 2, 4, 3, 0, 4, 9, 0, 6, 5, 7, 9, 8, 6, 5,
    7, 8,
)


def dot(left, right, dims):
    return lax.dot_general(left, right, dims, preferred_element_type=F32)


def gelu_and_slope(upper):
    cdf = 0.5 * (1.0 + lax.erf(upper * 2.0**-0.5))
    density = jnp.exp2((-0.5 * LOG2E) * (upper * upper)) * (2.0 * jnp.pi) ** -0.5
    return upper * cdf, cdf + upper * density


def layer_norm(values):
    centre = values - jnp.mean(values, axis=-1, keepdims=True)
    inverse = lax.rsqrt(jnp.mean(centre * centre, axis=-1, keepdims=True) + EPS)
    return centre * inverse, inverse


def norm_back(grad_out, normal, inverse, gain):
    scaled = grad_out * gain
    return inverse * (
        scaled
        - jnp.mean(scaled, axis=-1, keepdims=True)
        - normal * jnp.mean(scaled * normal, axis=-1, keepdims=True)
    )


def kernel(
    ndp,
    inputs_ref, lengths_ref, cot_ref, pool_ref,
    qkv_hbm, qb_ref, vb_ref, out_hbm, ob_ref, g1_ref, b1_ref,
    up_hbm, ub_ref, down_hbm, db_ref, g2_ref, b2_ref,
    block_ref, pooled_ref, igrad_ref, full, wide, small_ref,
    x, cot, qkv_w, out_w, up_w, down_w, qkv_t,
    q_t, kd_t, kz_t, v_x, probs, inv, c_t, y1, r1, first_low, active, slope,
    lower, gsum, g_low, g_up, g_hid, gc_t, gj_t, bout, igr, pool,
    part, small, late, up_row,
    w_sem, loc_sem, in_send, in_recv, out_send, out_recv, pool_send, pool_recv,
    s_a, s_b, gs_t, gs_n, p_n, *travel_refs,
):
    dp = lax.axis_index("dp")
    sq = lax.axis_index("seq")
    core = lax.rem(sq, 2)
    yy = lax.div(sq, 2)
    xx = lax.rem(dp, 2)
    zz = lax.rem(lax.div(dp, 2), 4)
    extra = []
    bit = 8
    while bit < ndp:
        extra.append(bit)
        bit *= 2

    def flip(index, amount):
        digit = lax.rem(lax.div(index, amount), 2)
        return index + amount * (1 - 2 * digit)

    seq_peers = [lax.rem(sq + step, 4) for step in (1, 2, 3)]
    core_peer = (dp, flip(sq, 1))
    y_peer = (dp, flip(sq, 2))
    x_peer = (flip(dp, 1), sq)
    xy_peer = (flip(dp, 1), flip(sq, 2))
    z_peers = [(dp + 2 * (lax.rem(zz + step, 4) - zz), sq) for step in (1, 2, 3)]
    w_peers = [(flip(dp, amount), sq) for amount in extra]
    greeted = [(dp, peer) for peer in seq_peers] + [x_peer, xy_peer] + z_peers + w_peers
    halvings = {
        "core": (core, core_peer),
        "y": (yy, y_peer),
        "x": (xx, x_peer),
        "z1": (lax.rem(zz, 2), (flip(dp, 2), sq)),
        "z2": (lax.div(zz, 2), (flip(dp, 4), sq)),
        "p": (
            xx + core * (yy - xx),
            (dp + (1 - core) * (flip(dp, 1) - dp), sq + core * (flip(sq, 2) - sq)),
        ),
        "q": (
            yy + core * (xx - yy),
            (dp + core * (flip(dp, 1) - dp), sq + (1 - core) * (flip(sq, 2) - sq)),
        ),
    }

    loads = [
        pltpu.make_async_copy(src, dst, w_sem.at[i])
        for i, (src, dst) in enumerate(
            [(qkv_hbm, qkv_w), (out_hbm, out_w), (up_hbm, up_w), (down_hbm, down_w)]
        )
    ]
    for load in loads:
        load.start()
    own_rows = pl.ds(pl.multiple_of(sq * 128, 128), 128)
    own_x = pltpu.make_async_copy(inputs_ref.at[sq, 0], x.at[own_rows], loc_sem.at[0])
    own_c = pltpu.make_async_copy(cot_ref.at[sq, 0], cot.at[own_rows], loc_sem.at[1])
    own_x.start()
    own_c.start()

    barrier = pltpu.get_barrier_semaphore()
    for peer in greeted:
        pl.semaphore_signal(barrier, inc=1, device_id=peer, device_id_type=MESH)
    pl.semaphore_wait(barrier, len(greeted))

    def remote(src, dst, send, recv, peer):
        return pltpu.make_async_remote_copy(
            src_ref=src, dst_ref=dst, send_sem=send, recv_sem=recv,
            device_id=peer, device_id_type=MESH,
        )

    x_moves, c_moves = [], []
    for which, (src, dst, moves) in enumerate(((inputs_ref, x, x_moves), (cot_ref, cot, c_moves))):
        for i, peer in enumerate(seq_peers):
            move = remote(
                src.at[peer, 0], dst.at[own_rows],
                in_send.at[which, i], in_recv.at[which, i], (dp, peer),
            )
            moves.append(move)
    for move in x_moves:
        move.start()

    span = lengths_ref[0, sq]
    query_bias, value_bias, out_bias, gain_one, bias_one, up_bias, down_bias, gain_two, bias_two = (
        ref[...].reshape(1, -1)
        for ref in (qb_ref, vb_ref, ob_ref, g1_ref, b1_ref, ub_ref, db_ref, g2_ref, b2_ref)
    )
    up_row[...] = up_bias
    count = span.astype(F32)
    lane_valid = lax.broadcasted_iota(jnp.int32, (1, 512), 1) < span

    loads[0].wait()

    for i in range(3):
        for g in range(GROUPS):
            turned = qkv_w[:, i * D + g * 128 : i * D + (g + 1) * 128].T
            for j in range(2):
                first = (2 * g + j) * 192 + i * 64
                qkv_t[first : first + 64, :] = turned[j * 64 : (j + 1) * 64]
    own_x.wait()
    for move in x_moves:
        move.wait()
    for move in c_moves:
        move.start()

    qcol = jnp.broadcast_to(query_bias, (8, D)).T[:, :1]
    vcol = jnp.broadcast_to(value_bias, (8, D)).T[:, :1]
    ones_row = jnp.broadcast_to(jnp.where(lane_valid, 1.0, 0.0), (16, 512)).astype(BF16)
    for g in range(GROUPS):
        joined = dot(qkv_t[g * D : (g + 1) * D, :], x[...], NT)
        for j in range(2):
            feats = slice((2 * g + j) * 64, (2 * g + j + 1) * 64)
            first = j * 192
            q_t[feats, :] = (joined[first : first + 64] + qcol[feats]).astype(BF16)
            keys = joined[first + 64 : first + 128]
            kd_t[feats, :] = jnp.where(lane_valid, keys, keys[:, :1]).astype(BF16)
            kz_t[feats, :] = jnp.where(lane_valid, keys, 0.0).astype(BF16)
            values = jnp.where(lane_valid, joined[first + 128 : first + 192] + vcol[feats], 0.0).astype(BF16)
            for i in range(2):
                h = 4 * g + 2 * j + i
                v_x[h * VROWS : h * VROWS + HD, :] = values[i * HD : (i + 1) * HD, :]
                v_x[h * VROWS + HD : (h + 1) * VROWS, :] = ones_row

    def score(h):
        rows = slice(h * HD, (h + 1) * HD)
        return dot(kd_t[rows, :], q_t[rows, :], TN)

    def soften(scores):
        peak = jnp.max(scores, axis=0, keepdims=True)
        return jnp.exp2(scores * (SCALE * LOG2E) - peak * (SCALE * LOG2E)).astype(BF16)

    def gather(h, raised):
        both = dot(v_x[h * VROWS : (h + 1) * VROWS, :], raised, NN)
        inverse = 1.0 / both[HD : HD + 1, :]
        inv[h] = jnp.broadcast_to(inverse, (8, 512))
        c_t[h * HD : (h + 1) * HD, :] = (both[:HD, :] * inverse).astype(BF16)

    sbufs = (s_a, s_b)
    s_a[...] = score(0)
    for h in range(H):
        if h + 1 < H:
            sbufs[(h + 1) % 2][...] = score(h + 1)
        for q in range(4):
            probs[h, :, q * 128 : (q + 1) * 128] = soften(sbufs[h % 2][:, q * 128 : (q + 1) * 128])
        gather(h, probs[h])

    loads[1].wait()

    lower[...] = dot(c_t[...], out_w[...], TN)

    def norm_one(i):
        rows = slice(i * 128, (i + 1) * 128)
        normal, inverse = layer_norm(x[rows, :].astype(F32) + lower[rows, :] + out_bias)
        y1[rows, :] = normal
        r1[rows, :] = inverse
        first_low[rows, :] = (normal * gain_one + bias_one).astype(BF16)

    for i in range(4):
        norm_one(i)
    loads[2].wait()

    def raise_up(i):
        cols = slice(i * 256, (i + 1) * 256)
        upper = dot(first_low[...], up_w[:, cols], NN) + up_row[:, cols]
        act, slp = gelu_and_slope(upper)
        active[:, cols] = act.astype(BF16)
        slope[:, cols] = slp

    for i in range(FF // 256):
        raise_up(i)
    loads[3].wait()
    lower[...] = dot(active[...], down_w[...], NN)
    own_c.wait()
    for move in c_moves:
        move.wait()
    chosen = lax.broadcasted_iota(jnp.int32, (4, D), 0) == sq
    pool_share = jnp.sum(jnp.where(chosen, pool_ref[0].astype(F32), 0.0), axis=0, keepdims=True) / count

    zero_row = jnp.zeros((1, D), F32)

    def norm_two(i, carry):
        sums, gain_sum, bias_sum, down_sum = carry
        rows = slice(i * 128, (i + 1) * 128)
        firsts = y1[rows, :] * gain_one + bias_one
        normal, inverse = layer_norm(firsts + lower[rows, :] + down_bias)
        here = lax.broadcasted_iota(jnp.int32, (128, 1), 0) + i * 128 < span
        masked = jnp.where(here, normal * gain_two + bias_two, 0.0)
        bout[rows, :] = masked.astype(BF16)
        grad = jnp.where(here, cot[rows, :].astype(F32) + pool_share, 0.0)
        grad_in = norm_back(grad, normal, inverse, gain_two)
        gsum[rows, :] = grad_in
        low = grad_in.astype(BF16)
        g_low[rows, :] = low
        return (
            sums + jnp.sum(masked, axis=0, keepdims=True),
            gain_sum + jnp.sum(grad * normal, axis=0, keepdims=True),
            bias_sum + jnp.sum(grad, axis=0, keepdims=True),
            down_sum + jnp.sum(low.astype(F32), axis=0, keepdims=True),
        )

    carry = (zero_row, zero_row, zero_row, zero_row)
    for i in range(4):
        carry = norm_two(i, carry)
    sums, gain2, bias2, down_sum = carry
    pool[sq] = jnp.broadcast_to(sums / count, (8, D))
    small[4:5, :] = down_sum
    small[10:11, :] = gain2
    small[11:12, :] = bias2

    out_moves = []
    for i, peer in enumerate(seq_peers):
        move = remote(
            bout.at[pl.ds(pl.multiple_of(peer * 128, 128), 128)], block_ref.at[sq, 0],
            out_send.at[0, i], out_recv.at[0, i], (dp, peer),
        )
        move.start()
        out_moves.append(move)
        move = remote(pool.at[sq], pool.at[sq], pool_send.at[i], pool_recv.at[i], (dp, peer))
        move.start()
        out_moves.append(move)
    own_b = pltpu.make_async_copy(bout.at[own_rows], block_ref.at[sq, 0], loc_sem.at[2])
    own_b.start()

    def add(left, right):
        return (left.astype(F32) + right.astype(F32)).astype(BF16)

    def piece(base, size):
        return pl.ds(base if isinstance(base, int) else pl.multiple_of(base, 16), size)

    plane = 2 * yy + xx
    plane_peers = [(x_peer, yy * 2 + 1 - xx), (y_peer, (1 - yy) * 2 + xx), (xy_peer, (1 - yy) * 2 + 1 - xx)]
    z_places = [(peer, lax.rem(zz + 1 + j, 4)) for j, peer in enumerate(z_peers)]
    groups = {name: (digit, [(peer, 1 - digit)]) for name, (digit, peer) in halvings.items()}
    groups["xy"] = (plane, plane_peers)
    groups["z"] = groups["all_z"] = (zz, z_places)
    at_end = lax.rem(zz, 3) == 0
    z_pair = (dp + 2 * (flip(zz, 1) - zz), sq)
    z_across = (dp + 2 * (3 - 2 * zz), sq)
    refs = list(travel_refs)

    def travel(first, rows, way):
        levels = len(way)
        gots = [refs.pop(0) for _ in range(levels)]
        sums = [refs.pop(0) for _ in range(levels - 1)]
        more = refs.pop(0) if w_peers else None
        send, recv = refs.pop(0), refs.pop(0)
        return steps_of(first, rows, way, gots, sums, more, send, recv)

    def steps_of(first, rows, way, gots, sums, more, send, recv):
        used = iter(range(100))
        held, offset, base, size = part, first, first, rows
        places = []
        for level, name in enumerate(way):
            if name == "line":
                mine, spot = held.at[piece(offset, size)], full.at[piece(base, size)]
                got = gots[level]
                inward, across, outward = (
                    remote(src, dst, send.at[n], recv.at[n], peer)
                    for n, src, dst, peer in (
                        (next(used), mine, got.at[0], z_pair),
                        (next(used), got.at[2], got.at[1], z_across),
                        (next(used), spot, spot, z_pair),
                    )
                )

                @pl.when(at_end)
                def _():
                    inward.start()

                yield

                @pl.when(at_end)
                def _():
                    inward.wait_send()

                @pl.when(jnp.logical_not(at_end))
                def _():
                    inward.wait_recv()
                    got[2] = add(mine[...], got[0])
                    across.start()

                yield

                @pl.when(jnp.logical_not(at_end))
                def _():
                    across.wait()
                    full[piece(base, size), :] = add(got[2], got[1])
                    outward.start()

                yield

                @pl.when(at_end)
                def _():
                    outward.wait_recv()

                @pl.when(jnp.logical_not(at_end))
                def _():
                    outward.wait_send()

                continue
            index, peers = groups[name]
            moves = []
            if name == "all_z":
                gots[level][index] = held[piece(offset, size), :]
                mine = gots[level].at[index]
                for peer, _ in peers:
                    n = next(used)
                    moves.append(remote(mine, mine, send.at[n], recv.at[n], peer))
            else:
                size //= len(peers) + 1
                for j, (peer, where) in enumerate(peers):
                    n = next(used)
                    moves.append(remote(
                        held.at[piece(offset + where * size, size)], gots[level].at[j],
                        send.at[n], recv.at[n], peer,
                    ))
            for move in moves:
                move.start()
            yield
            for move in moves:
                move.wait()
            if name == "all_z":
                terms = [gots[level][j].astype(F32) for j in range(4)]
                total = (terms[0] + terms[1]) + (terms[2] + terms[3])
            else:
                total = held[piece(offset + index * size, size), :].astype(F32)
                for j in range(len(peers)):
                    total = total + gots[level][j].astype(F32)
                base = base + index * size
                places.append((base, size, peers))
            if level < len(way) - 1:
                sums[level][...] = total.astype(BF16)
                held, offset = sums[level], 0
            else:
                full[piece(base, size), :] = total.astype(BF16)
        for e, peer in enumerate(w_peers):
            n = next(used)
            spot = full.at[piece(base, size)]
            move = remote(spot, more.at[e], send.at[n], recv.at[n], peer)
            move.start()
            move.wait()
            full[piece(base, size), :] = add(full[piece(base, size), :], more[e])
        for base, size, peers in reversed(places):
            moves = []
            for peer, _ in peers:
                n = next(used)
                spot = full.at[piece(base, size)]
                moves.append(remote(spot, spot, send.at[n], recv.at[n], peer))
            for move in moves:
                move.start()
            yield
            for move in moves:
                move.wait()
        last = min(first + rows, WIDE)
        if first < last:
            wide[first:last, :] = full[first:last, :].astype(F32)

    def vectors(mine, got, planes, zs, more, send, recv):
        move = remote(mine, got, send.at[0], recv.at[0], core_peer)
        move.start()
        yield
        move.wait()
        total = mine[...] + got[...]
        for slots, index, peers, n in ((planes, plane, plane_peers, 1), (zs, zz, z_places, 4)):
            slots[index] = total
            moves = [
                remote(slots.at[index], slots.at[index], send.at[n + j], recv.at[n + j], peer)
                for j, (peer, _) in enumerate(peers)
            ]
            for move in moves:
                move.start()
            yield
            for move in moves:
                move.wait()
            total = (slots[0] + slots[1]) + (slots[2] + slots[3])
        mine[...] = total
        for e, peer in enumerate(w_peers):
            move = remote(mine, more.at[e], send.at[7 + e], recv.at[7 + e], peer)
            move.start()
            move.wait()
            mine[...] = mine[...] + more[e]

    def back_home():
        for i, peer in enumerate(seq_peers):
            move = remote(
                igr.at[pl.ds(pl.multiple_of(peer * 128, 128), 128)], igrad_ref.at[sq, 0],
                out_send.at[1, i], out_recv.at[1, i], (dp, peer),
            )
            move.start()
            out_moves.append(move)
        yield

    def vector_refs():
        got, planes, zs = refs.pop(0), refs.pop(0), refs.pop(0)
        more = refs.pop(0) if w_peers else None
        return got, planes, zs, more, refs.pop(0), refs.pop(0)

    travels = [travel(*entry) for entry in PLAN]
    travels += [vectors(small, *vector_refs()), vectors(late, *vector_refs()), back_home()]
    agenda = list(SCHEDULE)

    def go():
        while agenda and agenda[0] >= 0:
            next(travels[agenda.pop(0)], None)
        if agenda:
            agenda.pop(0)

    def launch(n):
        next(travels[n])

    for i in range(3):
        part[i * 512 : (i + 1) * 512, :] = dot(
            active[:, i * 512 : (i + 1) * 512], g_low[...], TN
        ).astype(BF16)
        launch(i)
        go()

    for j in range(3):
        for i in (2 * j, 2 * j + 1):
            cols = slice(i * 256, (i + 1) * 256)
            g_up[:, cols] = (dot(g_low[...], down_w[cols, :], NT) * slope[:, cols]).astype(BF16)
        go()
    for i in range(4):
        small[i : i + 1, :] = jnp.sum(
            g_up[:, i * D : (i + 1) * D].astype(F32), axis=0, keepdims=True
        )
        part[ROWS + i * D : ROWS + (i + 1) * D, :] = dot(
            first_low[...], g_up[:, i * D : (i + 1) * D], TN
        ).astype(BF16)
    for i in range(3):
        launch(3 + i)
    go()
    lower[...] = dot(g_up[...], up_w[...], NT)
    go()

    def norm_one_back(i, carry):
        gain_sum, bias_sum, out_sum = carry
        rows = slice(i * 128, (i + 1) * 128)
        grad = gsum[rows, :] + lower[rows, :]
        normal = y1[rows, :]
        grad_in = norm_back(grad, normal, r1[rows, :], gain_one)
        g_hid[rows, :] = grad_in
        low = grad_in.astype(BF16)
        g_low[rows, :] = low
        return (
            gain_sum + jnp.sum(grad * normal, axis=0, keepdims=True),
            bias_sum + jnp.sum(grad, axis=0, keepdims=True),
            out_sum + jnp.sum(low.astype(F32), axis=0, keepdims=True),
        )

    carry = (zero_row, zero_row, zero_row)
    for i in range(4):
        carry = norm_one_back(i, carry)
    gain1, bias1, out_sum = carry
    small[5:6, :] = out_sum
    small[8:9, :] = gain1
    small[9:10, :] = bias1
    small[6:8, :] = jnp.zeros((2, D), F32)
    small[12:16, :] = jnp.zeros((4, D), F32)
    launch(len(PLAN))
    go()

    part[2 * ROWS : 2 * ROWS + D, :] = dot(c_t[...], g_low[...], NN).astype(BF16)
    gc_t[...] = dot(out_w[...], g_low[...], NT).astype(BF16)
    go()

    def scale_c(h):
        rows = slice(h * HD, (h + 1) * HD)
        return (gc_t[rows, :].astype(F32) * inv[h][:1, :]).astype(BF16)

    def grad_weights(h):
        sbufs[h % 2][...] = dot(v_x[h * VROWS : h * VROWS + HD, :], scale_c(h), TN)

    grad_weights(0)

    def attend_back(h):
        rows = slice(h * HD, (h + 1) * HD)
        if h + 1 < H:
            grad_weights(h + 1)
        grad_c = scale_c(h)
        inner = jnp.sum(grad_c.astype(F32) * c_t[rows, :].astype(F32), axis=0, keepdims=True)
        weights = probs[h]
        gs_t[...] = (weights.astype(F32) * (sbufs[h % 2][...] - inner)).astype(BF16)
        gs_n[...] = gs_t[...].T
        p_n[...] = weights.T
        base = (h // 2) * 192 + (h % 2) * HD
        gv = jnp.where(lane_valid, dot(grad_c, p_n[...], NN), 0.0)
        gj_t[base + 128 : base + 128 + HD, :] = gv.astype(BF16)
        gj_t[base : base + HD, :] = (dot(kz_t[rows, :], gs_t[...], NN) * SCALE).astype(BF16)
        gk = jnp.where(lane_valid, dot(q_t[rows, :], gs_n[...], NN) * SCALE, 0.0)
        gj_t[base + 64 : base + 64 + HD, :] = gk.astype(BF16)

    for h in range(H):
        attend_back(h)
        if h % 2 == 1:
            first = (h // 2) * 192
            begin = 2 * ROWS + D + first
            part[begin : begin + 192, :] = dot(gj_t[first : first + 192, :], x[...], NN).astype(BF16)
            ready = begin + 192
            for n in range(6, len(PLAN)):
                if ready - 192 < PLAN[n][0] + PLAN[n][1] <= ready:
                    launch(n)
        go()
    query_sums, value_sums = [], []
    for g in range(H // 2):
        both = dot(jnp.ones((16, 512), BF16), gj_t[g * 192 : (g + 1) * 192, :], NT)
        query_sums.append(both[:1, :64])
        value_sums.append(both[:1, 128:])
    late[...] = jnp.concatenate(
        [
            jnp.concatenate(query_sums, axis=1),
            jnp.concatenate(value_sums, axis=1),
            jnp.zeros((6, D), F32),
        ],
        axis=0,
    )
    launch(len(PLAN) + 1)
    go()

    igr[...] = (g_hid[...] + dot(gj_t[...], qkv_t[...], TN)).astype(BF16)
    own_i = pltpu.make_async_copy(igr.at[own_rows], igrad_ref.at[sq, 0], loc_sem.at[3])
    own_i.start()
    go()

    go()
    small_ref[...] = small[...]
    small_ref[6:8, :] = late[:2, :]
    for move in out_moves:
        move.wait()
    pooled_ref[...] = pool[...]
    own_b.wait()
    own_i.wait()


def finish_kernel(
    grads_ref, wide_ref, small_ref, pool_ref, bl_ref, ig_ref,
    block_ref, pooled_ref, igrad_ref, qkv_ref, qb_ref, vb_ref, out_ref, ob_ref, g1_ref, b1_ref,
    up_ref, ub_ref, down_ref, db_ref, g2_ref, b2_ref,
    qkv_wide, sem,
):
    copies = [(wide_ref.at[pl.ds(0, FF)], down_ref)]
    copies += [
        (wide_ref.at[pl.ds(FF + i * D, D)], up_ref.at[:, pl.ds(i * D, D)]) for i in range(4)
    ]
    copies += [(wide_ref.at[pl.ds(2 * FF, D)], out_ref), (bl_ref, block_ref), (ig_ref, igrad_ref)]
    moves = []
    for i, (src, dst) in enumerate(copies):
        move = pltpu.make_async_copy(src, dst, sem.at[i])
        move.start()
        moves.append(move)
    for i in range(3):
        first = WIDE + i * 64
        turned = [grads_ref[first + g * 192 : first + g * 192 + 64, :] for g in range(H // 2)]
        qkv_wide[i] = jnp.concatenate(turned, axis=0).T.astype(F32)
        move = pltpu.make_async_copy(
            qkv_wide.at[i], qkv_ref.at[:, pl.ds(i * D, D)], sem.at[len(copies) + i]
        )
        move.start()
        moves.append(move)
    for i in range(4):
        ub_ref[i * D : (i + 1) * D] = small_ref[i, :]
    for m in range(4):
        pooled_ref[m] = pool_ref[m, :1, :]
    for row, ref in ((4, db_ref), (5, ob_ref), (6, qb_ref), (7, vb_ref), (8, g1_ref), (9, b1_ref), (10, g2_ref), (11, b2_ref)):
        ref[...] = small_ref[row, :]
    for move in moves:
        move.wait()


def travel_scratch(rows, way, extra):
    gots, sums, count = [], [], extra
    for name in way:
        peers = {"xy": 3, "z": 3, "all_z": 3}.get(name, 1)
        if name == "line":
            gots.append(pltpu.VMEM((3, rows, D), BF16))
            count += 3
        elif name == "all_z":
            gots.append(pltpu.VMEM((4, rows, D), BF16))
            count += 3
        else:
            rows //= peers + 1
            gots.append(pltpu.VMEM((peers, rows, D), BF16))
            count += 2 * peers
        sums.append(pltpu.VMEM((rows, D), BF16))
    more = [pltpu.VMEM((extra, rows, D), BF16)] if extra else []
    return gots + sums[:-1] + more + [pltpu.SemaphoreType.DMA((count,))] * 2


def vector_scratch(rows, extra):
    slots = [pltpu.VMEM((rows, D), F32), pltpu.VMEM((4, rows, D), F32), pltpu.VMEM((4, rows, D), F32)]
    more = [pltpu.VMEM((extra, rows, D), F32)] if extra else []
    return slots + more + [pltpu.SemaphoreType.DMA((7 + extra,))] * 2


def body(
    ndp,
    inputs, lengths, cotangent, pool_cotangent, qkv_weight, query_bias, value_bias,
    out_weight, out_bias, norm1_gain, norm1_bias, up_weight, up_bias, down_weight,
    down_bias, norm2_gain, norm2_bias,
):
    any_spec = pl.BlockSpec(memory_space=pltpu.HBM)
    vmem = pl.BlockSpec(memory_space=pltpu.VMEM)
    smem = pl.BlockSpec(memory_space=pltpu.SMEM)
    extra = max(ndp.bit_length() - 4, 0)

    def v(*shape, dtype=BF16):
        return pltpu.VMEM(shape, dtype)

    dma = pltpu.SemaphoreType.DMA
    args = (
        inputs, lengths.T, cotangent, jnp.transpose(pool_cotangent, (1, 0, 2)),
        qkv_weight, query_bias, value_bias, out_weight, out_bias,
        norm1_gain, norm1_bias, up_weight, up_bias, down_weight, down_bias,
        norm2_gain, norm2_bias,
    )
    in_specs = [
        any_spec, smem, any_spec, vmem,
        any_spec, vmem, vmem, any_spec, vmem,
        vmem, vmem, any_spec, vmem, any_spec, vmem,
        vmem, vmem,
    ]
    results = pl.pallas_call(
        functools.partial(kernel, ndp),
        out_shape=(
            v(*inputs.shape), v(4, 8, D, dtype=F32), v(*inputs.shape), v(CHUNKS * ROWS, D), v(WIDE, D, dtype=F32), v(16, D, dtype=F32),
        ),
        in_specs=in_specs,
        out_specs=(vmem,) * 6,
        scratch_shapes=[
            v(512, D), v(512, D), v(D, 3 * D), v(D, D), v(D, FF), v(FF, D), v(3 * D, D),
            v(D, 512), v(D, 512), v(D, 512), v(H * VROWS, 512), v(H, 512, 512), v(H, 8, 512, dtype=F32),
            v(D, 512), v(512, D, dtype=F32), v(512, 1, dtype=F32), v(512, D), v(512, FF), v(512, FF, dtype=F32),
            v(512, D, dtype=F32), v(512, D, dtype=F32), v(512, D), v(512, FF), v(512, D, dtype=F32),
            v(D, 512), v(3 * D, 512), v(512, D), v(512, D), v(4, 8, D, dtype=F32),
            v(CHUNKS * ROWS, D),
            v(16, D, dtype=F32), v(8, D, dtype=F32), v(1, FF, dtype=F32),
            dma((4,)), dma((4,)), dma((2, 3)), dma((2, 3)), dma((2, 3)), dma((2, 3)), dma((3,)), dma((3,)),
            v(512, 512, dtype=F32), v(512, 512, dtype=F32), v(512, 512), v(512, 512), v(512, 512),
            *[item for _, rows, way in PLAN for item in travel_scratch(rows, way, extra)],
            *[item for rows in (16, 8) for item in vector_scratch(rows, extra)],
        ],
        compiler_params=pltpu.CompilerParams(
            collective_id=0, has_side_effects=True, vmem_limit_bytes=52 * 2**20
        ),
    )(*args)
    block, pooled, igrad, grads, wide, small = results

    def shape(*dims, dtype=F32):
        return jax.ShapeDtypeStruct(dims, dtype)

    outs = pl.pallas_call(
        finish_kernel,
        out_shape=(
            shape(*inputs.shape, dtype=BF16), shape(4, 1, D), shape(*inputs.shape, dtype=BF16),
            shape(D, 3 * D), shape(D), shape(D), shape(D, D), shape(D), shape(D), shape(D),
            shape(D, FF), shape(FF), shape(FF, D), shape(D), shape(D), shape(D),
        ),
        in_specs=[vmem] * 6,
        out_specs=(
            any_spec, vmem, any_spec, any_spec, vmem, vmem, any_spec, vmem, vmem, vmem,
            any_spec, vmem, any_spec, vmem, vmem, vmem,
        ),
        scratch_shapes=[v(3, D, D, dtype=F32), dma((11,))],
        compiler_params=pltpu.CompilerParams(vmem_limit_bytes=8 * 2**20),
    )(grads, wide, small, pooled, block, igrad)
    return outs


def solution(mesh):
    whole = P()
    return jax.shard_map(
        functools.partial(body, mesh.shape["dp"]),
        mesh=mesh,
        in_specs=(
            P(None, "dp", "seq", None), P(None, "dp"), P(None, "dp", "seq", None), P(None, "dp", None),
        ) + (whole,) * 13,
        out_specs=(
            P(None, "dp", "seq", None), P(None, "dp", None), P(None, "dp", "seq", None),
        ) + (whole,) * 13,
        check_vma=False,
    )
```

```python
import functools

import jax
import jax.numpy as jnp
from jax import lax
from jax.experimental import pallas as pl
from jax.experimental.pallas import tpu as pltpu
from jax.sharding import PartitionSpec as P

H = 12
HD = 32
D = 384
FF = 1536
EPS = 1e-6
F32 = jnp.float32
BF16 = jnp.bfloat16
MESH = pl.DeviceIdType.MESH
NN = (((1,), (0,)), ((), ()))
NT = (((1,), (1,)), ((), ()))
TN = (((0,), (0,)), ((), ()))
LOG2E = 1.4426950408889634
SCALE = HD**-0.5
VROWS = HD + 16
CHUNKS = 3
ROWS = 1536
GROUPS = 3
WIDE = 2 * ROWS + D
PLAN = (
    (0, 512, ("core", "z1", "p", "q", "z2")),
    (512, 512, ("core", "p", "q", "z")),
    (1024, 512, ("core", "z1", "xy", "z2")),
    (1536, 512, ("core", "p", "q", "line")),
    (2048, 512, ("core", "p", "q", "z1", "z2")),
    (2560, 512, ("core", "z1", "z2", "xy")),
    (3072, 512, ("core", "p", "q", "line")),
    (3584, 256, ("core", "p", "q", "line")),
    (3840, 256, ("core", "p", "q", "line")),
    (4096, 256, ("core", "xy", "line")),
    (4352, 256, ("core", "xy", "all_z")),
)
SCHEDULE = (
    -1, -1, -1, 0, -1, 2, 1, -1, -1, -1, -1, 3, 4, 5, 0, -1, 1, 11, -1, 2, -1, -1, 3, -1, 5, 4, 6, 0,
    1, -1, 7, -1, 11, -1, -1, 4, 3, 2, -1, 6, 8, 0, 7, -1, 5, -1, -1, 4, 9, 6, 3, 1, -1, 8, 7, 10, -1,
    13, 5, 0, 2, 12, 11, 4, 6, 3, 8, 9, 7, 10, 1, 0, 2, 4, 3, 6, 8, 7, 9, 5, 12, 1, 0, 4, 8, 6, 9, 10,
    7, 2, 3, 1, 0, 8, 4, 5, 9, 6, 1, 7, 12, 10, 2, 3, 8, 10, 2, 4, 3, 0, 4, 9, 0, 6, 5, 7, 9, 8, 6, 5,
    7, 8,
)


def dot(left, right, dims):
    return lax.dot_general(left, right, dims, preferred_element_type=F32)


def gelu_and_slope(upper):
    cdf = 0.5 * (1.0 + lax.erf(upper * 2.0**-0.5))
    density = jnp.exp2((-0.5 * LOG2E) * (upper * upper)) * (2.0 * jnp.pi) ** -0.5
    return upper * cdf, cdf + upper * density


def layer_norm(values):
    centre = values - jnp.mean(values, axis=-1, keepdims=True)
    inverse = lax.rsqrt(jnp.mean(centre * centre, axis=-1, keepdims=True) + EPS)
    return centre * inverse, inverse


def norm_back(grad_out, normal, inverse, gain):
    scaled = grad_out * gain
    return inverse * (
        scaled
        - jnp.mean(scaled, axis=-1, keepdims=True)
        - normal * jnp.mean(scaled * normal, axis=-1, keepdims=True)
    )


def kernel(
    ndp,
    inputs_ref, lengths_ref, cot_ref, pool_ref,
    qkv_hbm, qb_ref, vb_ref, out_hbm, ob_ref, g1_ref, b1_ref,
    up_hbm, ub_ref, down_hbm, db_ref, g2_ref, b2_ref,
    block_ref, pooled_ref, igrad_ref, full, wide, small_ref,
    x, cot, qkv_w, out_w, up_w, down_w, qkv_t,
    q_t, kd_t, kz_t, v_x, probs, inv, c_t, y1, r1, first_low, active, slope,
    lower, gsum, g_low, g_up, g_hid, gc_t, gj_t, bout, igr, pool,
    part, small, late, up_row, vecs, up_vec, pool_in, vec_sem,
    w_sem, loc_sem, in_send, in_recv, out_send, out_recv, pool_send, pool_recv,
    s_a, s_b, gs_t, gs_n, p_n, *travel_refs,
):
    dp = lax.axis_index("dp")
    sq = lax.axis_index("seq")
    core = lax.rem(sq, 2)
    yy = lax.div(sq, 2)
    xx = lax.rem(dp, 2)
    zz = lax.rem(lax.div(dp, 2), 4)
    extra = []
    bit = 8
    while bit < ndp:
        extra.append(bit)
        bit *= 2

    def flip(index, amount):
        digit = lax.rem(lax.div(index, amount), 2)
        return index + amount * (1 - 2 * digit)

    seq_peers = [lax.rem(sq + step, 4) for step in (1, 2, 3)]
    core_peer = (dp, flip(sq, 1))
    y_peer = (dp, flip(sq, 2))
    x_peer = (flip(dp, 1), sq)
    xy_peer = (flip(dp, 1), flip(sq, 2))
    z_peers = [(dp + 2 * (lax.rem(zz + step, 4) - zz), sq) for step in (1, 2, 3)]
    w_peers = [(flip(dp, amount), sq) for amount in extra]
    greeted = [(dp, peer) for peer in seq_peers] + [x_peer, xy_peer] + z_peers + w_peers
    halvings = {
        "core": (core, core_peer),
        "y": (yy, y_peer),
        "x": (xx, x_peer),
        "z1": (lax.rem(zz, 2), (flip(dp, 2), sq)),
        "z2": (lax.div(zz, 2), (flip(dp, 4), sq)),
        "p": (
            xx + core * (yy - xx),
            (dp + (1 - core) * (flip(dp, 1) - dp), sq + core * (flip(sq, 2) - sq)),
        ),
        "q": (
            yy + core * (xx - yy),
            (dp + core * (flip(dp, 1) - dp), sq + (1 - core) * (flip(sq, 2) - sq)),
        ),
    }

    barrier = pltpu.get_barrier_semaphore()
    for peer in greeted:
        pl.semaphore_signal(barrier, inc=1, device_id=peer, device_id_type=MESH)
    loads = [
        pltpu.make_async_copy(src, dst, w_sem.at[i])
        for i, (src, dst) in enumerate(
            [(qkv_hbm, qkv_w), (out_hbm, out_w), (up_hbm, up_w), (down_hbm, down_w)]
        )
    ]
    for load in loads:
        load.start()
    own_rows = pl.ds(pl.multiple_of(sq * 128, 128), 128)
    own_x = pltpu.make_async_copy(inputs_ref.at[sq, 0], x.at[own_rows], loc_sem.at[0])
    own_c = pltpu.make_async_copy(cot_ref.at[sq, 0], cot.at[own_rows], loc_sem.at[1])
    own_x.start()
    vec_refs = (qb_ref, vb_ref, ob_ref, g1_ref, b1_ref, db_ref, g2_ref, b2_ref)
    vec_moves = [pltpu.make_async_copy(src, dst, vec_sem.at[i]) for i, (src, dst) in enumerate(zip(vec_refs, vecs))]
    vec_moves.append(pltpu.make_async_copy(ub_ref, up_vec, vec_sem.at[8]))
    vec_moves.append(pltpu.make_async_copy(pool_ref, pool_in, vec_sem.at[9]))
    for move in vec_moves:
        move.start()
    own_c.start()

    pl.semaphore_wait(barrier, len(greeted))

    def remote(src, dst, send, recv, peer):
        return pltpu.make_async_remote_copy(
            src_ref=src, dst_ref=dst, send_sem=send, recv_sem=recv,
            device_id=peer, device_id_type=MESH,
        )

    x_moves, c_moves = [], []
    for which, (src, dst, moves) in enumerate(((inputs_ref, x, x_moves), (cot_ref, cot, c_moves))):
        for i, peer in enumerate(seq_peers):
            move = remote(
                src.at[peer, 0], dst.at[own_rows],
                in_send.at[which, i], in_recv.at[which, i], (dp, peer),
            )
            moves.append(move)
    for move in x_moves:
        move.start()

    span = lengths_ref[0, sq]
    count = span.astype(F32)
    lane_valid = lax.broadcasted_iota(jnp.int32, (1, 512), 1) < span
    for move in vec_moves:
        move.wait()
    query_bias, value_bias, out_bias, gain_one, bias_one, down_bias, gain_two, bias_two = (
        vec[...].reshape(1, -1) for vec in vecs
    )
    up_row[...] = up_vec[...].reshape(1, -1)
    loads[0].wait()

    for i in range(3):
        for g in range(GROUPS):
            turned = qkv_w[:, i * D + g * 128 : i * D + (g + 1) * 128].T
            for j in range(2):
                first = (2 * g + j) * 192 + i * 64
                qkv_t[first : first + 64, :] = turned[j * 64 : (j + 1) * 64]
    own_x.wait()
    for move in x_moves:
        move.wait()
    for move in c_moves:
        move.start()

    qcol = jnp.broadcast_to(query_bias, (8, D)).T[:, :1]
    vcol = jnp.broadcast_to(value_bias, (8, D)).T[:, :1]
    ones_row = jnp.broadcast_to(jnp.where(lane_valid, 1.0, 0.0), (16, 512)).astype(BF16)
    for g in range(GROUPS):
        joined = dot(qkv_t[g * D : (g + 1) * D, :], x[...], NT)
        for j in range(2):
            feats = slice((2 * g + j) * 64, (2 * g + j + 1) * 64)
            first = j * 192
            q_t[feats, :] = (joined[first : first + 64] + qcol[feats]).astype(BF16)
            keys = joined[first + 64 : first + 128]
            kd_t[feats, :] = jnp.where(lane_valid, keys, keys[:, :1]).astype(BF16)
            kz_t[feats, :] = jnp.where(lane_valid, keys, 0.0).astype(BF16)
            values = jnp.where(lane_valid, joined[first + 128 : first + 192] + vcol[feats], 0.0).astype(BF16)
            for i in range(2):
                h = 4 * g + 2 * j + i
                v_x[h * VROWS : h * VROWS + HD, :] = values[i * HD : (i + 1) * HD, :]
                v_x[h * VROWS + HD : (h + 1) * VROWS, :] = ones_row

    def score(h):
        rows = slice(h * HD, (h + 1) * HD)
        return dot(kd_t[rows, :], q_t[rows, :], TN)

    def soften(scores):
        peak = jnp.max(scores, axis=0, keepdims=True)
        return jnp.exp2(scores * (SCALE * LOG2E) - peak * (SCALE * LOG2E)).astype(BF16)

    def gather(h, raised):
        both = dot(v_x[h * VROWS : (h + 1) * VROWS, :], raised, NN)
        inverse = 1.0 / both[HD : HD + 1, :]
        inv[h] = jnp.broadcast_to(inverse, (8, 512))
        c_t[h * HD : (h + 1) * HD, :] = (both[:HD, :] * inverse).astype(BF16)

    sbufs = (s_a, s_b)
    s_a[...] = score(0)
    for h in range(H):
        if h + 1 < H:
            sbufs[(h + 1) % 2][...] = score(h + 1)
        for q in range(4):
            probs[h, :, q * 128 : (q + 1) * 128] = soften(sbufs[h % 2][:, q * 128 : (q + 1) * 128])
        gather(h, probs[h])

    loads[1].wait()

    lower[...] = dot(c_t[...], out_w[...], TN)

    def norm_one(i):
        rows = slice(i * 128, (i + 1) * 128)
        normal, inverse = layer_norm(x[rows, :].astype(F32) + lower[rows, :] + out_bias)
        y1[rows, :] = normal
        r1[rows, :] = inverse
        first_low[rows, :] = (normal * gain_one + bias_one).astype(BF16)

    for i in range(4):
        norm_one(i)
    loads[2].wait()

    def raise_up(i):
        cols = slice(i * 256, (i + 1) * 256)
        upper = dot(first_low[...], up_w[:, cols], NN) + up_row[:, cols]
        act, slp = gelu_and_slope(upper)
        active[:, cols] = act.astype(BF16)
        slope[:, cols] = slp

    for i in range(FF // 256):
        raise_up(i)
    loads[3].wait()
    lower[...] = dot(active[...], down_w[...], NN)
    own_c.wait()
    for move in c_moves:
        move.wait()
    chosen = lax.broadcasted_iota(jnp.int32, (4, D), 0) == sq
    pool_share = jnp.sum(jnp.where(chosen, pool_in[0].astype(F32), 0.0), axis=0, keepdims=True) / count

    zero_row = jnp.zeros((1, D), F32)

    def norm_two(i, carry):
        sums, gain_sum, bias_sum, down_sum = carry
        rows = slice(i * 128, (i + 1) * 128)
        firsts = y1[rows, :] * gain_one + bias_one
        normal, inverse = layer_norm(firsts + lower[rows, :] + down_bias)
        here = lax.broadcasted_iota(jnp.int32, (128, 1), 0) + i * 128 < span
        masked = jnp.where(here, normal * gain_two + bias_two, 0.0)
        bout[rows, :] = masked.astype(BF16)
        grad = jnp.where(here, cot[rows, :].astype(F32) + pool_share, 0.0)
        grad_in = norm_back(grad, normal, inverse, gain_two)
        gsum[rows, :] = grad_in
        low = grad_in.astype(BF16)
        g_low[rows, :] = low
        return (
            sums + jnp.sum(masked, axis=0, keepdims=True),
            gain_sum + jnp.sum(grad * normal, axis=0, keepdims=True),
            bias_sum + jnp.sum(grad, axis=0, keepdims=True),
            down_sum + jnp.sum(low.astype(F32), axis=0, keepdims=True),
        )

    carry = (zero_row, zero_row, zero_row, zero_row)
    for i in range(4):
        carry = norm_two(i, carry)
    sums, gain2, bias2, down_sum = carry
    pool[sq] = jnp.broadcast_to(sums / count, (8, D))
    small[4:5, :] = down_sum
    small[10:11, :] = gain2
    small[11:12, :] = bias2

    out_moves = []
    for i, peer in enumerate(seq_peers):
        move = remote(
            bout.at[pl.ds(pl.multiple_of(peer * 128, 128), 128)], block_ref.at[sq, 0],
            out_send.at[0, i], out_recv.at[0, i], (dp, peer),
        )
        move.start()
        out_moves.append(move)
        move = remote(pool.at[sq], pool.at[sq], pool_send.at[i], pool_recv.at[i], (dp, peer))
        move.start()
        out_moves.append(move)
    own_b = pltpu.make_async_copy(bout.at[own_rows], block_ref.at[sq, 0], loc_sem.at[2])
    own_b.start()

    def add(left, right):
        return (left.astype(F32) + right.astype(F32)).astype(BF16)

    def piece(base, size):
        return pl.ds(base if isinstance(base, int) else pl.multiple_of(base, 16), size)

    plane = 2 * yy + xx
    plane_peers = [(x_peer, yy * 2 + 1 - xx), (y_peer, (1 - yy) * 2 + xx), (xy_peer, (1 - yy) * 2 + 1 - xx)]
    z_places = [(peer, lax.rem(zz + 1 + j, 4)) for j, peer in enumerate(z_peers)]
    groups = {name: (digit, [(peer, 1 - digit)]) for name, (digit, peer) in halvings.items()}
    groups["xy"] = (plane, plane_peers)
    groups["z"] = groups["all_z"] = (zz, z_places)
    at_end = lax.rem(zz, 3) == 0
    z_pair = (dp + 2 * (flip(zz, 1) - zz), sq)
    z_across = (dp + 2 * (3 - 2 * zz), sq)
    refs = list(travel_refs)

    def travel(first, rows, way):
        levels = len(way)
        gots = [refs.pop(0) for _ in range(levels)]
        sums = [refs.pop(0) for _ in range(levels - 1)]
        more = refs.pop(0) if w_peers else None
        send, recv = refs.pop(0), refs.pop(0)
        return steps_of(first, rows, way, gots, sums, more, send, recv)

    def steps_of(first, rows, way, gots, sums, more, send, recv):
        used = iter(range(100))
        held, offset, base, size = part, first, first, rows
        places = []
        for level, name in enumerate(way):
            if name == "line":
                mine, spot = held.at[piece(offset, size)], full.at[piece(base, size)]
                got = gots[level]
                inward, across, outward = (
                    remote(src, dst, send.at[n], recv.at[n], peer)
                    for n, src, dst, peer in (
                        (next(used), mine, got.at[0], z_pair),
                        (next(used), got.at[2], got.at[1], z_across),
                        (next(used), spot, spot, z_pair),
                    )
                )

                @pl.when(at_end)
                def _():
                    inward.start()

                yield

                @pl.when(at_end)
                def _():
                    inward.wait_send()

                @pl.when(jnp.logical_not(at_end))
                def _():
                    inward.wait_recv()
                    got[2] = add(mine[...], got[0])
                    across.start()

                yield

                @pl.when(jnp.logical_not(at_end))
                def _():
                    across.wait()
                    full[piece(base, size), :] = add(got[2], got[1])
                    outward.start()

                yield

                @pl.when(at_end)
                def _():
                    outward.wait_recv()

                @pl.when(jnp.logical_not(at_end))
                def _():
                    outward.wait_send()

                continue
            index, peers = groups[name]
            moves = []
            if name == "all_z":
                gots[level][index] = held[piece(offset, size), :]
                mine = gots[level].at[index]
                for peer, _ in peers:
                    n = next(used)
                    moves.append(remote(mine, mine, send.at[n], recv.at[n], peer))
            else:
                size //= len(peers) + 1
                for j, (peer, where) in enumerate(peers):
                    n = next(used)
                    moves.append(remote(
                        held.at[piece(offset + where * size, size)], gots[level].at[j],
                        send.at[n], recv.at[n], peer,
                    ))
            for move in moves:
                move.start()
            yield
            for move in moves:
                move.wait()
            if name == "all_z":
                terms = [gots[level][j].astype(F32) for j in range(4)]
                total = (terms[0] + terms[1]) + (terms[2] + terms[3])
            else:
                total = held[piece(offset + index * size, size), :].astype(F32)
                for j in range(len(peers)):
                    total = total + gots[level][j].astype(F32)
                base = base + index * size
                places.append((base, size, peers))
            if level < len(way) - 1:
                sums[level][...] = total.astype(BF16)
                held, offset = sums[level], 0
            else:
                full[piece(base, size), :] = total.astype(BF16)
        for e, peer in enumerate(w_peers):
            n = next(used)
            spot = full.at[piece(base, size)]
            move = remote(spot, more.at[e], send.at[n], recv.at[n], peer)
            move.start()
            move.wait()
            full[piece(base, size), :] = add(full[piece(base, size), :], more[e])
        for base, size, peers in reversed(places):
            moves = []
            for peer, _ in peers:
                n = next(used)
                spot = full.at[piece(base, size)]
                moves.append(remote(spot, spot, send.at[n], recv.at[n], peer))
            for move in moves:
                move.start()
            yield
            for move in moves:
                move.wait()
        last = min(first + rows, WIDE)
        if first < last:
            wide[first:last, :] = full[first:last, :].astype(F32)

    def vectors(mine, got, planes, zs, more, send, recv):
        move = remote(mine, got, send.at[0], recv.at[0], core_peer)
        move.start()
        yield
        move.wait()
        total = mine[...] + got[...]
        for slots, index, peers, n in ((planes, plane, plane_peers, 1), (zs, zz, z_places, 4)):
            slots[index] = total
            moves = [
                remote(slots.at[index], slots.at[index], send.at[n + j], recv.at[n + j], peer)
                for j, (peer, _) in enumerate(peers)
            ]
            for move in moves:
                move.start()
            yield
            for move in moves:
                move.wait()
            total = (slots[0] + slots[1]) + (slots[2] + slots[3])
        mine[...] = total
        for e, peer in enumerate(w_peers):
            move = remote(mine, more.at[e], send.at[7 + e], recv.at[7 + e], peer)
            move.start()
            move.wait()
            mine[...] = mine[...] + more[e]

    def back_home():
        for i, peer in enumerate(seq_peers):
            move = remote(
                igr.at[pl.ds(pl.multiple_of(peer * 128, 128), 128)], igrad_ref.at[sq, 0],
                out_send.at[1, i], out_recv.at[1, i], (dp, peer),
            )
            move.start()
            out_moves.append(move)
        yield

    def vector_refs():
        got, planes, zs = refs.pop(0), refs.pop(0), refs.pop(0)
        more = refs.pop(0) if w_peers else None
        return got, planes, zs, more, refs.pop(0), refs.pop(0)

    travels = [travel(*entry) for entry in PLAN]
    travels += [vectors(small, *vector_refs()), vectors(late, *vector_refs()), back_home()]
    agenda = list(SCHEDULE)

    def go():
        while agenda and agenda[0] >= 0:
            next(travels[agenda.pop(0)], None)
        if agenda:
            agenda.pop(0)

    def launch(n):
        next(travels[n])

    for i in range(3):
        part[i * 512 : (i + 1) * 512, :] = dot(
            active[:, i * 512 : (i + 1) * 512], g_low[...], TN
        ).astype(BF16)
        launch(i)
        go()

    for j in range(3):
        for i in (2 * j, 2 * j + 1):
            cols = slice(i * 256, (i + 1) * 256)
            g_up[:, cols] = (dot(g_low[...], down_w[cols, :], NT) * slope[:, cols]).astype(BF16)
        go()
    for i in range(4):
        small[i : i + 1, :] = jnp.sum(
            g_up[:, i * D : (i + 1) * D].astype(F32), axis=0, keepdims=True
        )
        part[ROWS + i * D : ROWS + (i + 1) * D, :] = dot(
            first_low[...], g_up[:, i * D : (i + 1) * D], TN
        ).astype(BF16)
    for i in range(3):
        launch(3 + i)
    go()
    lower[...] = dot(g_up[...], up_w[...], NT)
    go()

    def norm_one_back(i, carry):
        gain_sum, bias_sum, out_sum = carry
        rows = slice(i * 128, (i + 1) * 128)
        grad = gsum[rows, :] + lower[rows, :]
        normal = y1[rows, :]
        grad_in = norm_back(grad, normal, r1[rows, :], gain_one)
        g_hid[rows, :] = grad_in
        low = grad_in.astype(BF16)
        g_low[rows, :] = low
        return (
            gain_sum + jnp.sum(grad * normal, axis=0, keepdims=True),
            bias_sum + jnp.sum(grad, axis=0, keepdims=True),
            out_sum + jnp.sum(low.astype(F32), axis=0, keepdims=True),
        )

    carry = (zero_row, zero_row, zero_row)
    for i in range(4):
        carry = norm_one_back(i, carry)
    gain1, bias1, out_sum = carry
    small[5:6, :] = out_sum
    small[8:9, :] = gain1
    small[9:10, :] = bias1
    small[6:8, :] = jnp.zeros((2, D), F32)
    small[12:16, :] = jnp.zeros((4, D), F32)
    launch(len(PLAN))
    go()

    part[2 * ROWS : 2 * ROWS + D, :] = dot(c_t[...], g_low[...], NN).astype(BF16)
    gc_t[...] = dot(out_w[...], g_low[...], NT).astype(BF16)
    go()

    def scale_c(h):
        rows = slice(h * HD, (h + 1) * HD)
        return (gc_t[rows, :].astype(F32) * inv[h][:1, :]).astype(BF16)

    def grad_weights(h):
        sbufs[h % 2][...] = dot(v_x[h * VROWS : h * VROWS + HD, :], scale_c(h), TN)

    grad_weights(0)

    def attend_back(h):
        rows = slice(h * HD, (h + 1) * HD)
        if h + 1 < H:
            grad_weights(h + 1)
        grad_c = scale_c(h)
        inner = jnp.sum(grad_c.astype(F32) * c_t[rows, :].astype(F32), axis=0, keepdims=True)
        weights = probs[h]
        gs_t[...] = (weights.astype(F32) * (sbufs[h % 2][...] - inner)).astype(BF16)
        gs_n[...] = gs_t[...].T
        p_n[...] = weights.T
        base = (h // 2) * 192 + (h % 2) * HD
        gv = jnp.where(lane_valid, dot(grad_c, p_n[...], NN), 0.0)
        gj_t[base + 128 : base + 128 + HD, :] = gv.astype(BF16)
        gj_t[base : base + HD, :] = (dot(kz_t[rows, :], gs_t[...], NN) * SCALE).astype(BF16)
        gk = jnp.where(lane_valid, dot(q_t[rows, :], gs_n[...], NN) * SCALE, 0.0)
        gj_t[base + 64 : base + 64 + HD, :] = gk.astype(BF16)

    for h in range(H):
        attend_back(h)
        if h % 2 == 1:
            first = (h // 2) * 192
            begin = 2 * ROWS + D + first
            part[begin : begin + 192, :] = dot(gj_t[first : first + 192, :], x[...], NN).astype(BF16)
            ready = begin + 192
            for n in range(6, len(PLAN)):
                if ready - 192 < PLAN[n][0] + PLAN[n][1] <= ready:
                    launch(n)
        go()
    query_sums, value_sums = [], []
    for g in range(H // 2):
        both = dot(jnp.ones((16, 512), BF16), gj_t[g * 192 : (g + 1) * 192, :], NT)
        query_sums.append(both[:1, :64])
        value_sums.append(both[:1, 128:])
    late[...] = jnp.concatenate(
        [
            jnp.concatenate(query_sums, axis=1),
            jnp.concatenate(value_sums, axis=1),
            jnp.zeros((6, D), F32),
        ],
        axis=0,
    )
    launch(len(PLAN) + 1)
    go()

    igr[...] = (g_hid[...] + dot(gj_t[...], qkv_t[...], TN)).astype(BF16)
    own_i = pltpu.make_async_copy(igr.at[own_rows], igrad_ref.at[sq, 0], loc_sem.at[3])
    own_i.start()
    go()

    go()
    small_ref[...] = small[...]
    small_ref[6:8, :] = late[:2, :]
    for move in out_moves:
        move.wait()
    pooled_ref[...] = pool[...]
    own_b.wait()
    own_i.wait()


def finish_kernel(
    grads_ref, wide_ref, small_ref, pool_ref, bl_ref, ig_ref,
    block_ref, pooled_ref, igrad_ref, qkv_ref, qb_ref, vb_ref, out_ref, ob_ref, g1_ref, b1_ref,
    up_ref, ub_ref, down_ref, db_ref, g2_ref, b2_ref,
    qkv_wide, rows_1d, row_ub, row_pool, sem,
):
    moves = []
    for i in range(4):
        row_ub[i * D : (i + 1) * D] = small_ref[i, :]
    for m in range(4):
        row_pool[m] = pool_ref[m, :1, :]
    for i, (row, ref) in enumerate(
        ((4, db_ref), (5, ob_ref), (6, qb_ref), (7, vb_ref), (8, g1_ref), (9, b1_ref), (10, g2_ref), (11, b2_ref))
    ):
        rows_1d[i][...] = small_ref[row, :]
        moves.append(pltpu.make_async_copy(rows_1d[i], ref, sem.at[11 + i]))
    moves.append(pltpu.make_async_copy(row_ub, ub_ref, sem.at[19]))
    moves.append(pltpu.make_async_copy(row_pool, pooled_ref, sem.at[20]))
    for move in moves:
        move.start()
    copies = [(wide_ref.at[pl.ds(0, FF)], down_ref)]
    copies += [
        (wide_ref.at[pl.ds(FF + i * D, D)], up_ref.at[:, pl.ds(i * D, D)]) for i in range(4)
    ]
    copies += [(wide_ref.at[pl.ds(2 * FF, D)], out_ref), (bl_ref, block_ref), (ig_ref, igrad_ref)]
    for i, (src, dst) in enumerate(copies):
        move = pltpu.make_async_copy(src, dst, sem.at[i])
        move.start()
        moves.append(move)
    for i in range(3):
        first = WIDE + i * 64
        turned = [grads_ref[first + g * 192 : first + g * 192 + 64, :] for g in range(H // 2)]
        qkv_wide[i] = jnp.concatenate(turned, axis=0).T.astype(F32)
        move = pltpu.make_async_copy(
            qkv_wide.at[i], qkv_ref.at[:, pl.ds(i * D, D)], sem.at[len(copies) + i]
        )
        move.start()
        moves.append(move)
    for move in moves:
        move.wait()


def travel_scratch(rows, way, extra):
    gots, sums, count = [], [], extra
    for name in way:
        peers = {"xy": 3, "z": 3, "all_z": 3}.get(name, 1)
        if name == "line":
            gots.append(pltpu.VMEM((3, rows, D), BF16))
            count += 3
        elif name == "all_z":
            gots.append(pltpu.VMEM((4, rows, D), BF16))
            count += 3
        else:
            rows //= peers + 1
            gots.append(pltpu.VMEM((peers, rows, D), BF16))
            count += 2 * peers
        sums.append(pltpu.VMEM((rows, D), BF16))
    more = [pltpu.VMEM((extra, rows, D), BF16)] if extra else []
    return gots + sums[:-1] + more + [pltpu.SemaphoreType.DMA((count,))] * 2


def vector_scratch(rows, extra):
    slots = [pltpu.VMEM((rows, D), F32), pltpu.VMEM((4, rows, D), F32), pltpu.VMEM((4, rows, D), F32)]
    more = [pltpu.VMEM((extra, rows, D), F32)] if extra else []
    return slots + more + [pltpu.SemaphoreType.DMA((7 + extra,))] * 2


def body(
    ndp,
    inputs, lengths, cotangent, pool_cotangent, qkv_weight, query_bias, value_bias,
    out_weight, out_bias, norm1_gain, norm1_bias, up_weight, up_bias, down_weight,
    down_bias, norm2_gain, norm2_bias,
):
    any_spec = pl.BlockSpec(memory_space=pltpu.HBM)
    vmem = pl.BlockSpec(memory_space=pltpu.VMEM)
    smem = pl.BlockSpec(memory_space=pltpu.SMEM)
    extra = max(ndp.bit_length() - 4, 0)

    def v(*shape, dtype=BF16):
        return pltpu.VMEM(shape, dtype)

    dma = pltpu.SemaphoreType.DMA
    args = (
        inputs, lengths.T, cotangent, jnp.transpose(pool_cotangent, (1, 0, 2)),
        qkv_weight, query_bias, value_bias, out_weight, out_bias,
        norm1_gain, norm1_bias, up_weight, up_bias, down_weight, down_bias,
        norm2_gain, norm2_bias,
    )
    in_specs = [
        any_spec, smem,
    ] + [any_spec] * 15
    results = pl.pallas_call(
        functools.partial(kernel, ndp),
        out_shape=(
            v(*inputs.shape), v(4, 8, D, dtype=F32), v(*inputs.shape), v(CHUNKS * ROWS, D), v(WIDE, D, dtype=F32), v(16, D, dtype=F32),
        ),
        in_specs=in_specs,
        out_specs=(vmem,) * 6,
        scratch_shapes=[
            v(512, D), v(512, D), v(D, 3 * D), v(D, D), v(D, FF), v(FF, D), v(3 * D, D),
            v(D, 512), v(D, 512), v(D, 512), v(H * VROWS, 512), v(H, 512, 512), v(H, 8, 512, dtype=F32),
            v(D, 512), v(512, D, dtype=F32), v(512, 1, dtype=F32), v(512, D), v(512, FF), v(512, FF, dtype=F32),
            v(512, D, dtype=F32), v(512, D, dtype=F32), v(512, D), v(512, FF), v(512, D, dtype=F32),
            v(D, 512), v(3 * D, 512), v(512, D), v(512, D), v(4, 8, D, dtype=F32),
            v(CHUNKS * ROWS, D),
            v(16, D, dtype=F32), v(8, D, dtype=F32), v(1, FF, dtype=F32),
            [v(D, dtype=F32)] * 8, v(FF, dtype=F32), v(1, 4, D), dma((10,)),
            dma((4,)), dma((4,)), dma((2, 3)), dma((2, 3)), dma((2, 3)), dma((2, 3)), dma((3,)), dma((3,)),
            v(512, 512, dtype=F32), v(512, 512, dtype=F32), v(512, 512), v(512, 512), v(512, 512),
            *[item for _, rows, way in PLAN for item in travel_scratch(rows, way, extra)],
            *[item for rows in (16, 8) for item in vector_scratch(rows, extra)],
        ],
        compiler_params=pltpu.CompilerParams(
            collective_id=0, has_side_effects=True, vmem_limit_bytes=52 * 2**20
        ),
    )(*args)
    block, pooled, igrad, grads, wide, small = results

    def shape(*dims, dtype=F32):
        return jax.ShapeDtypeStruct(dims, dtype)

    outs = pl.pallas_call(
        finish_kernel,
        out_shape=(
            shape(*inputs.shape, dtype=BF16), shape(4, 1, D), shape(*inputs.shape, dtype=BF16),
            shape(D, 3 * D), shape(D), shape(D), shape(D, D), shape(D), shape(D), shape(D),
            shape(D, FF), shape(FF), shape(FF, D), shape(D), shape(D), shape(D),
        ),
        in_specs=[vmem] * 6,
        out_specs=(any_spec,) * 16,
        scratch_shapes=[
            v(3, D, D, dtype=F32), [v(D, dtype=F32)] * 8, v(FF, dtype=F32), v(4, 1, D, dtype=F32), dma((21,)),
        ],
        compiler_params=pltpu.CompilerParams(vmem_limit_bytes=8 * 2**20),
    )(grads, wide, small, pooled, block, igrad)
    return outs


def solution(mesh):
    whole = P()
    return jax.shard_map(
        functools.partial(body, mesh.shape["dp"]),
        mesh=mesh,
        in_specs=(
            P(None, "dp", "seq", None), P(None, "dp"), P(None, "dp", "seq", None), P(None, "dp", None),
        ) + (whole,) * 13,
        out_specs=(
            P(None, "dp", "seq", None), P(None, "dp", None), P(None, "dp", "seq", None),
        ) + (whole,) * 13,
        check_vma=False,
    )
```
